128 devices in a mesh: replica: 16 (over z, x_lo, core), shard: 8 (over y, x_hi).
Axes of the slice: x: 4 (x_hi: 2, x_lo: 2; x = x_hi * 2 + x_lo), y: 4, z: 4, core: 2. Of those that a mesh axis runs over, the one named last changes fastest.
Arguments:
- images: bfloat16 [768, 197, 384], P(('replica', 'shard')), may hold values from -6 to 6
- cotangent: bfloat16 [768, 197, 384], P(('replica', 'shard')), may hold values from -6 to 6
- image_count: int32 [128], P(('replica', 'shard')), may hold values from 1 to 6, as said below
- joint_weight: float32 [2, 384, 1152], P(None, 'shard'), may hold values from -0.3125 to 0.3125
- merge_weight: float32 [2, 384, 384], P(None, 'shard'), may hold values from -0.625 to 0.625
- expand_weight: float32 [2, 384, 1536], P(None, 'shard'), may hold values from -0.3125 to 0.3125
- reduce_weight: float32 [2, 1536, 384], P(None, 'shard'), may hold values from -0.15625 to 0.15625
- small_params: float32 [2, 3456], P(None, 'shard')
- joint_first: float32 [2, 384, 1152], P(None, 'shard')
- merge_first: float32 [2, 384, 384], P(None, 'shard')
- expand_first: float32 [2, 384, 1536], P(None, 'shard')
- reduce_first: float32 [2, 1536, 384], P(None, 'shard')
- small_first: float32 [2, 3456], P(None, 'shard')
- joint_second: float32 [2, 384, 1152], P(None, 'shard')
- merge_second: float32 [2, 384, 384], P(None, 'shard')
- expand_second: float32 [2, 384, 1536], P(None, 'shard')
- reduce_second: float32 [2, 1536, 384], P(None, 'shard')
- small_second: float32 [2, 3456], P(None, 'shard')
Outputs:
- block_out: float32 [768, 197, 384], P(('replica', 'shard'))
- image_grad: float32 [768, 197, 384], P(('replica', 'shard'))
- joint_grad: float32 [2, 384, 1152], P(None, 'shard')
- merge_grad: float32 [2, 384, 384], P(None, 'shard')
- expand_grad: float32 [2, 384, 1536], P(None, 'shard')
- reduce_grad: float32 [2, 1536, 384], P(None, 'shard')
- small_grad: float32 [2, 3456], P(None, 'shard')
- joint_mean: float32 [2, 384, 1152], P(None, 'shard')
- merge_mean: float32 [2, 384, 384], P(None, 'shard')
- expand_mean: float32 [2, 384, 1536], P(None, 'shard')
- reduce_mean: float32 [2, 1536, 384], P(None, 'shard')
- small_mean: float32 [2, 3456], P(None, 'shard')
- joint_square: float32 [2, 384, 1152], P(None, 'shard')
- merge_square: float32 [2, 384, 384], P(None, 'shard')
- expand_square: float32 [2, 384, 1536], P(None, 'shard')
- reduce_square: float32 [2, 1536, 384], P(None, 'shard')
- small_square: float32 [2, 3456], P(None, 'shard')
- joint_master: float32 [2, 384, 1152], P(None, 'shard')
- merge_master: float32 [2, 384, 384], P(None, 'shard')
- expand_master: float32 [2, 384, 1536], P(None, 'shard')
- reduce_master: float32 [2, 1536, 384], P(None, 'shard')
- small_master: float32 [2, 3456], P(None, 'shard')
The draws below stay inside these ranges and needn't reach their ends.
Inputs may be any that keep to these rules, and one draw needn't show every extreme that they name: `image_count`: the number of live images among a device's 6 slots; slots from that number on are empty; in every draw some device has 6 and some has 1.
All inputs are finite; a program needn't handle non-finite values.
Results may differ from the reference program's by a relative error of at most 0.015.
The reference program's roundings to bfloat16 on the way count: a program that leaves them out, or rounds other values in their place, can miss the bound.
Values may be sent and summed in bfloat16 or wider, within the bound.
A program may use at most 192 MiB of HBM per device.

```python
import math
import jax
import jax.numpy as jnp
from jax import lax

D = 384
FF = 1536
HEADS = 6
HD = 64
SEQ = 197
LAYERS = 2
STEP = 10
IMG_DEV = 6
IMAGES = 768
VEC = 3456


def grad_scale(coefficient):
    live_tokens = IMAGES * SEQ * (1 + IMG_DEV) / (2 * IMG_DEV)
    return coefficient * math.sqrt(live_tokens)


def attention_coefficient():
    return 1.0 / math.sqrt(SEQ)


def first_draw(key, full_shape, coefficient):
    return 0.11 * grad_scale(coefficient) * jax.random.normal(key, full_shape, jnp.float32)


def second_draw(key, full_shape, coefficient):
    level_key, spread_key = jax.random.split(key)
    level_factor = 2.0 ** jax.random.uniform(level_key, full_shape, jnp.float32, 0.0, 1.0)
    spread_factor = 2.0 ** jax.random.uniform(spread_key, full_shape, jnp.float32, -1.0, 1.0)
    magnitude = grad_scale(coefficient)
    return 0.001 * magnitude * magnitude * level_factor * spread_factor


def draw_image_count(key, part):
    key = jax.random.fold_in(key, 5)
    subkeys = jax.random.split(key, 3)
    devices_all = IMAGES // IMG_DEV
    counts = jax.random.randint(subkeys[0], (devices_all,), 1, IMG_DEV + 1)
    fullest = jax.random.randint(subkeys[1], (), 0, devices_all)
    emptiest = (fullest + jax.random.randint(subkeys[2], (), 1, devices_all)) % devices_all
    counts = counts.at[fullest].set(IMG_DEV)
    return counts.at[emptiest].set(1).astype(jnp.int32)


def draw_small_params(key, part):
    key = jax.random.fold_in(key, 7)
    subkeys = jax.random.split(key, 6)
    gain_one = 1.0 + 0.15 * jax.random.uniform(subkeys[0], (LAYERS, D), jnp.float32, -1.0, 1.0)
    shift_one = 0.2 * jax.random.normal(subkeys[1], (LAYERS, D), jnp.float32)
    gain_two = 1.0 + 0.15 * jax.random.uniform(subkeys[2], (LAYERS, D), jnp.float32, -1.0, 1.0)
    shift_two = 0.2 * jax.random.normal(subkeys[3], (LAYERS, D), jnp.float32)
    out_bias = 0.2 * jax.random.normal(subkeys[4], (LAYERS, D), jnp.float32)
    up_bias = 0.2 * jax.random.normal(subkeys[5], (LAYERS, FF), jnp.float32)
    return jnp.concatenate([gain_one, shift_one, gain_two, shift_two, out_bias, up_bias], axis=1)


def draw_joint_first(key, part):
    key = jax.random.fold_in(key, 11)
    return first_draw(key, (LAYERS, D, 3 * D), attention_coefficient())


def draw_merge_first(key, part):
    key = jax.random.fold_in(key, 12)
    return first_draw(key, (LAYERS, D, D), attention_coefficient())


def draw_expand_first(key, part):
    key = jax.random.fold_in(key, 13)
    return first_draw(key, (LAYERS, D, FF), 0.3)


def draw_reduce_first(key, part):
    key = jax.random.fold_in(key, 14)
    return first_draw(key, (LAYERS, FF, D), 0.6)


def draw_small_first(key, part):
    key = jax.random.fold_in(key, 15)
    return first_draw(key, (LAYERS, VEC), 0.7)


def draw_joint_second(key, part):
    key = jax.random.fold_in(key, 21)
    return second_draw(key, (LAYERS, D, 3 * D), attention_coefficient())


def draw_merge_second(key, part):
    key = jax.random.fold_in(key, 22)
    return second_draw(key, (LAYERS, D, D), attention_coefficient())


def draw_expand_second(key, part):
    key = jax.random.fold_in(key, 23)
    return second_draw(key, (LAYERS, D, FF), 0.3)


def draw_reduce_second(key, part):
    key = jax.random.fold_in(key, 24)
    return second_draw(key, (LAYERS, FF, D), 0.6)


def draw_small_second(key, part):
    key = jax.random.fold_in(key, 25)
    return second_draw(key, (LAYERS, VEC), 0.7)


def level_of(rng, dims, shards, least, top_value):
    gain = 1.0
    for dim, blocks in shards:
        draws = jax.random.uniform(jax.random.fold_in(jax.random.fold_in(rng, 6), dim), (blocks,), jnp.float32, least / len(shards), top_value / len(shards))
        gain = gain * jnp.repeat(jnp.exp(draws), dims[dim] // blocks).reshape((-1,) + (1,) * (len(dims) - 1 - dim))
    return gain


def bell_draw(rng, dims, scale, limit, cuts=(), held_as=jnp.bfloat16):
    drawn = scale * jax.random.normal(rng, dims, jnp.float32)
    if cuts:
        drawn = drawn * level_of(rng, dims, cuts, -0.22, 0.18)
    return jnp.clip(drawn, -limit, limit).astype(held_as)


def setup_inputs(seed: int = 0) -> dict:
    seeds = jax.random.split(jax.random.key(seed), 19)
    images = bell_draw(seeds[0], (IMAGES, SEQ, D), 1.0, 6.0, ((0, 128),))
    cotangent = bell_draw(seeds[1], (IMAGES, SEQ, D), 1.0, 6.0, ((0, 128),))
    image_count = draw_image_count(jax.random.fold_in(seeds[18], 71), 0)
    joint_weight = bell_draw(seeds[3], (LAYERS, D, 3 * D), D ** -0.5, 0.3125, ((1, 8),), jnp.float32)
    merge_weight = bell_draw(seeds[4], (LAYERS, D, D), (D // 4) ** -0.5, 0.625, ((1, 8),), jnp.float32)
    expand_weight = bell_draw(seeds[5], (LAYERS, D, FF), D ** -0.5, 0.3125, ((1, 8),), jnp.float32)
    reduce_weight = bell_draw(seeds[6], (LAYERS, FF, D), FF ** -0.5, 0.15625, ((1, 8),), jnp.float32)
    small_params = draw_small_params(jax.random.fold_in(seeds[18], 71), 0)
    joint_first = draw_joint_first(jax.random.fold_in(seeds[18], 71), 0)
    merge_first = draw_merge_first(jax.random.fold_in(seeds[18], 71), 0)
    expand_first = draw_expand_first(jax.random.fold_in(seeds[18], 71), 0)
    reduce_first = draw_reduce_first(jax.random.fold_in(seeds[18], 71), 0)
    small_first = draw_small_first(jax.random.fold_in(seeds[18], 71), 0)
    joint_second = draw_joint_second(jax.random.fold_in(seeds[18], 71), 0)
    merge_second = draw_merge_second(jax.random.fold_in(seeds[18], 71), 0)
    expand_second = draw_expand_second(jax.random.fold_in(seeds[18], 71), 0)
    reduce_second = draw_reduce_second(jax.random.fold_in(seeds[18], 71), 0)
    small_second = draw_small_second(jax.random.fold_in(seeds[18], 71), 0)
    return dict(images=images, cotangent=cotangent, image_count=image_count, joint_weight=joint_weight, merge_weight=merge_weight, expand_weight=expand_weight, reduce_weight=reduce_weight, small_params=small_params, joint_first=joint_first, merge_first=merge_first, expand_first=expand_first, reduce_first=reduce_first, small_first=small_first, joint_second=joint_second, merge_second=merge_second, expand_second=expand_second, reduce_second=reduce_second, small_second=small_second)


NORM_EPS = 1e-06
BETA_ONE = 0.9
BETA_TWO = 0.999
ADAM_EPS = 1e-08
DECAY_MATRIX = 0.05
RATE_MATRIX = 0.05
RATE_SMALL = 0.4
HIGH = lax.Precision.HIGHEST

@jax.custom_vjp
def low(v):
    return lax.optimization_barrier(v.astype(jnp.bfloat16)).astype(jnp.float32)

@jax.custom_vjp
def low_back(v):
    return v

def low_keep(v):
    return (low(v), None)

def low_pass(kept, grad):
    return (grad,)

def back_keep(v):
    return (v, None)

def back_low(kept, grad):
    return (low(grad),)
low.defvjp(low_keep, low_pass)
low_back.defvjp(back_keep, back_low)

def layer_norm(inputs, gain_vec, shift_vec):
    centered = inputs - lax.optimization_barrier(jnp.mean(inputs, axis=-1, keepdims=True))
    variance = lax.optimization_barrier(jnp.mean(centered * centered, axis=-1, keepdims=True))
    return centered * lax.rsqrt(variance + NORM_EPS) * gain_vec + shift_vec

def residual_block(stream, joint, merge, expand, reduce_w, vector):
    image_slots = stream.shape[0]
    vector_parts = [vector[position * D:(position + 1) * D] for position in range(5)] + [vector[5 * D:]]
    normed = low(layer_norm(stream, vector_parts[0], vector_parts[1]))
    mixed_rows = low_back(low(jnp.einsum('isd,de->ise', normed, joint, precision=HIGH)))
    query_rows = mixed_rows[..., :D].reshape(image_slots, SEQ, HEADS, HD)
    key_rows = mixed_rows[..., D:2 * D].reshape(image_slots, SEQ, HEADS, HD)
    value_rows = mixed_rows[..., 2 * D:].reshape(image_slots, SEQ, HEADS, HD)
    scores = low_back(jnp.einsum('iqhe,ikhe->ihqk', query_rows, key_rows, precision=HIGH) * HD ** (-0.5))
    row_top = lax.optimization_barrier(jnp.max(scores, axis=-1, keepdims=True))
    exponent = jnp.exp(scores - row_top)
    soft_weights = low(exponent / lax.optimization_barrier(jnp.sum(exponent, axis=-1, keepdims=True)))
    attended = low_back(low(jnp.einsum('ihqk,ikhe->iqhe', soft_weights, value_rows, precision=HIGH)))
    attended = attended.reshape(image_slots, SEQ, D)
    middle = stream + low_back(jnp.einsum('isd,de->ise', attended, merge, precision=HIGH))
    second_normed = low(layer_norm(middle, vector_parts[2], vector_parts[3]))
    hidden = low_back(jnp.einsum('isd,df->isf', second_normed, expand, precision=HIGH) + vector_parts[5])
    active = low(jax.nn.gelu(hidden, approximate=False))
    return middle + low_back(jnp.einsum('isf,fd->isd', active, reduce_w, precision=HIGH) + vector_parts[4])

def network(masters, stream):
    rounded = [low(member) for member in masters]
    for layer_index in range(LAYERS):
        stream = residual_block(stream, *[member[layer_index] for member in rounded])
    return stream

def adam_update(gradient, first_moment, second_moment, master, step_rate, decay_rate):
    first_new = BETA_ONE * first_moment + (1.0 - BETA_ONE) * gradient
    second_new = BETA_TWO * second_moment + (1.0 - BETA_TWO) * gradient * gradient
    corrected = first_new / (1.0 - BETA_ONE ** STEP)
    denominator = jnp.sqrt(second_new / (1.0 - BETA_TWO ** STEP)) + ADAM_EPS
    master_new = master - step_rate * (corrected / denominator + decay_rate * master)
    return (first_new, second_new, master_new)

def reference(images, cotangent, image_count, joint_weight, merge_weight, expand_weight, reduce_weight, small_params, joint_first, merge_first, expand_first, reduce_first, small_first, joint_second, merge_second, expand_second, reduce_second, small_second):
    masters = (joint_weight, merge_weight, expand_weight, reduce_weight, small_params)
    slot_index = jnp.arange(IMAGES, dtype=jnp.int32)
    owner_count = jnp.repeat(image_count, IMG_DEV, total_repeat_length=IMAGES)
    live_mask = (slot_index % IMG_DEV < owner_count).astype(jnp.float32)
    groups = IMAGES // 16
    stream_all = images.astype(jnp.float32).reshape(groups, 16, SEQ, D)
    back_all = (cotangent.astype(jnp.float32) * live_mask[:, None, None]).reshape(groups, 16, SEQ, D)
    live_all = live_mask.reshape(groups, 16)

    def group_step(carry, inputs):
        stream, back_rows, alive = inputs
        result, pullback = jax.vjp(network, masters, stream)
        param_grads, stream_grad = pullback(back_rows)
        carry = tuple((total + member for total, member in zip(carry, param_grads)))
        return (carry, (result * alive[:, None, None], stream_grad))
    zero_sums = tuple((jnp.zeros(member.shape, jnp.float32) for member in masters))
    grad_sums, (block_rows, grad_rows) = lax.scan(group_step, zero_sums, (stream_all, back_all, live_all))
    block_out = block_rows.reshape(IMAGES, SEQ, D)
    image_grad = grad_rows.reshape(IMAGES, SEQ, D)
    joint_mean, joint_square, joint_master = adam_update(grad_sums[0], joint_first, joint_second, joint_weight, RATE_MATRIX, DECAY_MATRIX)
    merge_mean, merge_square, merge_master = adam_update(grad_sums[1], merge_first, merge_second, merge_weight, RATE_MATRIX, DECAY_MATRIX)
    expand_mean, expand_square, expand_master = adam_update(grad_sums[2], expand_first, expand_second, expand_weight, RATE_MATRIX, DECAY_MATRIX)
    reduce_mean, reduce_square, reduce_master = adam_update(grad_sums[3], reduce_first, reduce_second, reduce_weight, RATE_MATRIX, DECAY_MATRIX)
    small_mean, small_square, small_master = adam_update(grad_sums[4], small_first, small_second, small_params, RATE_SMALL, 0.0)
    return (block_out, image_grad, grad_sums[0], grad_sums[1], grad_sums[2], grad_sums[3], grad_sums[4], joint_mean, merge_mean, expand_mean, reduce_mean, small_mean, joint_square, merge_square, expand_square, reduce_square, small_square, joint_master, merge_master, expand_master, reduce_master, small_master)
```

```python
import jax
import jax.numpy as jnp
from jax import lax
from jax.experimental import pallas as pl
from jax.experimental.pallas import tpu as pltpu
from jax.sharding import PartitionSpec as P

D = 384
FF = 1536
BLK = 640
F32 = jnp.float32
BF16 = jnp.bfloat16
HD = 64
NI = 6
SEQ = 197
R = 208
T = NI * R
CH = 416
NCH = T // CH
NORM_EPS = 1e-6


def dot(a, b):
    return lax.dot_general(a, b, (((1,), (0,)), ((), ())), preferred_element_type=F32)


def dot_nt(a, b):
    return lax.dot_general(a, b, (((1,), (1,)), ((), ())), preferred_element_type=F32)


def dot_tn(a, b):
    return lax.dot_general(a, b, (((0,), (0,)), ((), ())), preferred_element_type=F32)


def normalize(v):
    centered = v - jnp.mean(v, axis=-1, keepdims=True)
    variance = jnp.mean(centered * centered, axis=-1, keepdims=True)
    rstd = lax.rsqrt(variance + NORM_EPS)
    return centered * rstd, rstd


def gelu_pair(u):
    z = jnp.abs(u)
    d = 1.0 + (0.3275911 * 0.7071067811865476) * z
    t = 1.0 / d
    e = jnp.exp(-0.5 * (u * u))
    poly = ((((0.5 * 1.061405429) * t - 0.5 * 1.453152027) * t + 0.5 * 1.421413741) * t
            - 0.5 * 0.284496736) * t + 0.5 * 0.254829592
    half = poly * t * e
    phi = jnp.where(u < 0, half, 1.0 - half)
    return u * phi, phi + u * (e * 0.3989422804014327)


def norm_back(dy, xhat, rstd, gain):
    dxh = dy * gain
    m1 = jnp.mean(dxh, axis=-1, keepdims=True)
    m2 = jnp.mean(dxh * xhat, axis=-1, keepdims=True)
    return rstd * (dxh - m1 - xhat * m2)


def compute_kernel(count, img, cot, w_all, sp, out, dimg, g_all,
                   wj, wm, we, wr, xs, hs, a_s, c_s, o_s, qkv, g_s, gp_s, dx_s, dzb_s, dyb_s,
                   dob_s, lse_s, grad, small, wsem, gsem):
    def rows_of(c):
        return pl.ds(pl.multiple_of(c * CH, CH), CH)

    def img_rows(i, n=R):
        return pl.ds(pl.multiple_of(i * R, R), n)

    def weight_copies(l):
        out_list = []
        for cb in range(3):
            out_list.append((w_all.at[l, :, pl.ds(48 * cb, 48), :],
                             wj.at[l, :, :, pl.ds(D * cb, D)], 0))
        out_list.append((w_all.at[l, :, pl.ds(144, 48), :], wm.at[l], 1))
        for cb in range(4):
            out_list.append((w_all.at[l, :, pl.ds(192 + 48 * cb, 48), :],
                             we.at[l, :, :, pl.ds(D * cb, D)], 2))
        out_list.append((w_all.at[l, :, pl.ds(384, 192), :], wr.at[l], 3))
        return [pltpu.make_async_copy(s, d, wsem.at[l, k]) for k, (s, d, _) in enumerate(out_list)]

    copies = [weight_copies(0), weight_copies(1)]
    for l in range(2):
        for cp in copies[l]:
            cp.start()

    n_live = count[0]

    def load(i, _):
        live = jnp.where(i < n_live, 1.0, 0.0).astype(F32)
        tail = pl.ds(pl.multiple_of(i * R, R) + 192, 16)
        xs[0, tail, :] = jnp.zeros((16, D), F32)
        dx_s[tail, :] = jnp.zeros((16, D), F32)
        xs[0, img_rows(i, SEQ), :] = img[i].astype(F32)
        dx_s[img_rows(i, SEQ), :] = cot[i].astype(F32) * live
        return 0

    lax.fori_loop(0, NI, load, 0)

    lane = lax.broadcasted_iota(jnp.int32, (R, 128), 1)
    key_ok = lax.broadcasted_iota(jnp.int32, (R, R), 0) < SEQ

    def half(v, e):
        keep = (lane < HD) if e == 0 else (lane >= HD)
        return jnp.where(keep, v, jnp.zeros_like(v))

    for l in range(2):
        vec = lambda r: sp[l, r:r + 1, :]
        for cp in copies[l][:3]:
            cp.wait()

        def p1(c, _):
            rows = rows_of(c)
            xhat, _r = normalize(xs[l, rows, :])
            a = (xhat * vec(0) + vec(1)).astype(BF16)
            a_s[l, rows, :] = a
            for cb in range(3):
                part = dot(a, wj[l, :, :, pl.ds(D * cb, D)].reshape(D, D))
                if cb == 0:
                    part = part * (HD ** -0.5)
                qkv[l, rows, pl.ds(D * cb, D)] = part.astype(BF16)
            return 0

        lax.fori_loop(0, NCH, p1, 0)

        def p2(i, _):
            rows = img_rows(i)
            for j in range(3):
                q2 = qkv[l, rows, pl.ds(128 * j, 128)]
                k2 = qkv[l, rows, pl.ds(D + 128 * j, 128)]
                v2 = qkv[l, rows, pl.ds(2 * D + 128 * j, 128)]
                v2t = v2.T
                parts = []
                for e in range(2):
                    st = dot_nt(k2, half(q2, e))
                    st = jnp.where(key_ok, st, -1e30)
                    m = jnp.max(st, axis=0, keepdims=True)
                    pt = jnp.exp(st - m)
                    tot = jnp.sum(pt, axis=0, keepdims=True)
                    pbt = (pt * (1.0 / tot)).astype(BF16)
                    lse_s[l, i, 2 * j + e:2 * j + e + 1, :] = m + jnp.log(tot)
                    parts.append(dot(v2t[HD * e:HD * (e + 1), :], pbt))
                o_s[l, rows, pl.ds(128 * j, 128)] = jnp.concatenate(parts, axis=0).T.astype(BF16)
            return 0

        lax.fori_loop(0, NI, p2, 0)

        for cp in copies[l][3:]:
            cp.wait()

        def p3(c, _):
            rows = rows_of(c)
            h = xs[l, rows, :] + dot(o_s[l, rows, :], wm[l].reshape(D, D))
            hs[l, rows, :] = h
            xhat, _r = normalize(h)
            cc = (xhat * vec(2) + vec(3)).astype(BF16)
            c_s[l, rows, :] = cc
            acc = h + vec(4)
            for f in range(4):
                u = dot(cc, we[l, :, :, pl.ds(D * f, D)].reshape(D, D)) + vec(5 + f)
                g, gp = gelu_pair(u)
                g = g.astype(BF16)
                g_s[l, rows, pl.ds(D * f, D)] = g
                gp_s[l, rows, pl.ds(D * f, D)] = gp.astype(BF16)
                acc = acc + dot(g, wr[l, 2 * f:2 * f + 2].reshape(D, D))
            if l == 0:
                xs[1, rows, :] = acc
            else:
                for k in range(CH // R):
                    i = c * (CH // R) + k
                    live = jnp.where(i < n_live, 1.0, 0.0).astype(F32)
                    out[i] = acc[R * k:R * k + SEQ, :] * live
            return 0

        lax.fori_loop(0, NCH, p3, 0)

    small[...] = jnp.zeros_like(small)

    def colsum(v):
        return jnp.sum(v, axis=0, keepdims=True)

    for l in (1, 0):
        vec = lambda r: sp[l, r:r + 1, :]

        def b1(c, _):
            rows = rows_of(c)
            dx = dx_s[rows, :]
            dzb = dx.astype(BF16)
            dzb_s[rows, :] = dzb
            small[l, 4:5, :] += colsum(dzb.astype(F32))
            dc = None
            for f in range(4):
                dg = dot_nt(dzb, wr[l, 2 * f:2 * f + 2].reshape(D, D))
                du = (dg * gp_s[l, rows, pl.ds(D * f, D)].astype(F32)).astype(BF16)
                gp_s[l, rows, pl.ds(D * f, D)] = du
                small[l, 5 + f:6 + f, :] += colsum(du.astype(F32))
                part = dot_nt(du, we[l, :, :, pl.ds(D * f, D)].reshape(D, D))
                dc = part if dc is None else dc + part
            xhat, rstd = normalize(hs[l, rows, :])
            small[l, 2:3, :] += colsum(dc * xhat)
            small[l, 3:4, :] += colsum(dc)
            dh = dx + norm_back(dc, xhat, rstd, vec(2))
            dx_s[rows, :] = dh
            dyb = dh.astype(BF16)
            dyb_s[rows, :] = dyb
            dob_s[rows, :] = dot_nt(dyb, wm[l].reshape(D, D)).astype(BF16)
            return 0

        lax.fori_loop(0, NCH, b1, 0)

        def b2(i, _):
            rows = img_rows(i)
            for j in range(3):
                q2 = qkv[l, rows, pl.ds(128 * j, 128)]
                k2 = qkv[l, rows, pl.ds(D + 128 * j, 128)]
                v2 = qkv[l, rows, pl.ds(2 * D + 128 * j, 128)]
                do2 = dob_s[rows, pl.ds(128 * j, 128)]
                k2t = k2.T
                dv = dk = None
                dqt = []
                for e in range(2):
                    qe = half(q2, e)
                    de = half(do2, e)
                    st = dot_nt(k2, qe)
                    pt = jnp.where(key_ok, jnp.exp(st - lse_s[l, i, 2 * j + e:2 * j + e + 1, :]), 0.0)
                    dpt = dot_nt(v2, de)
                    r = jnp.sum(dpt * pt, axis=0, keepdims=True)
                    dst = (pt * (dpt - r)).astype(BF16)
                    dve = dot(pt.astype(BF16), de)
                    dke = dot(dst, qe)
                    dv = dve if dv is None else dv + dve
                    dk = dke if dk is None else dk + dke
                    dqt.append(dot(k2t[HD * e:HD * (e + 1), :], dst))
                dq = jnp.concatenate(dqt, axis=0).T * (HD ** -0.5)
                qkv[l, rows, pl.ds(128 * j, 128)] = dq.astype(BF16)
                qkv[l, rows, pl.ds(D + 128 * j, 128)] = dk.astype(BF16)
                qkv[l, rows, pl.ds(2 * D + 128 * j, 128)] = dv.astype(BF16)
            return 0

        lax.fori_loop(0, NI, b2, 0)

        def b3(c, _):
            rows = rows_of(c)
            da = None
            for cb in range(3):
                part = dot_nt(qkv[l, rows, pl.ds(D * cb, D)],
                              wj[l, :, :, pl.ds(D * cb, D)].reshape(D, D))
                da = part if da is None else da + part
            xhat, rstd = normalize(xs[l, rows, :])
            small[l, 0:1, :] += colsum(da * xhat)
            small[l, 1:2, :] += colsum(da)
            dx = dx_s[rows, :] + norm_back(da, xhat, rstd, vec(0))
            if l == 1:
                dx_s[rows, :] = dx
            else:
                for k in range(CH // R):
                    dimg[c * (CH // R) + k] = dx[R * k:R * k + SEQ, :]
            return 0

        lax.fori_loop(0, NCH, b3, 0)

        def shard_store(at, rows, val):
            grad[l, :, pl.ds(at, rows), :] = val.astype(BF16).reshape(8, rows, D)

        for cb in range(3):
            shard_store(48 * cb, 48, dot_tn(a_s[l], qkv[l, :, pl.ds(D * cb, D)]))
        shard_store(144, 48, dot_tn(o_s[l], dyb_s[...]))
        for f in range(4):
            shard_store(192 + 48 * f, 48, dot_tn(c_s[l], gp_s[l, :, pl.ds(D * f, D)]))
        for f in range(4):
            val = dot_tn(dzb_s[...], g_s[l, :, pl.ds(D * f, D)])
            grad[l, 2 * f:2 * f + 2, pl.ds(384, 192), :] = val.T.astype(BF16).reshape(2, 192, D)
        for s in range(8):
            grad[l, s, pl.ds(576, 16), :] = small[l].astype(BF16)
        pltpu.make_async_copy(grad.at[l], g_all.at[l], gsem.at[l]).start()
    for l in (1, 0):
        pltpu.make_async_copy(grad.at[l], g_all.at[l], gsem.at[l]).wait()


def compute(count, img, cot, w_all, sp):
    V = pl.BlockSpec(memory_space=pltpu.VMEM)
    A = pl.BlockSpec(memory_space=pl.ANY)
    vm = pltpu.VMEM
    return pl.pallas_call(
        compute_kernel,
        out_shape=(
            jax.ShapeDtypeStruct((NI, SEQ, D), F32),
            jax.ShapeDtypeStruct((NI, SEQ, D), F32),
            jax.ShapeDtypeStruct((2, 8, BLK, D), BF16),
        ),
        in_specs=[pl.BlockSpec(memory_space=pltpu.SMEM), V, V, A, V],
        out_specs=(V, V, A),
        scratch_shapes=[
            vm((2, 8, 48, 3 * D), BF16), vm((2, 8, 48, D), BF16), vm((2, 8, 48, FF), BF16),
            vm((2, 8, 192, D), BF16),
            vm((2, T, D), F32), vm((2, T, D), F32),
            vm((2, T, D), BF16), vm((2, T, D), BF16), vm((2, T, D), BF16),
            vm((2, T, 3 * D), BF16), vm((2, T, FF), BF16), vm((2, T, FF), BF16),
            vm((T, D), F32), vm((T, D), BF16), vm((T, D), BF16), vm((T, D), BF16),
            vm((2, NI, 8, R), F32),
            vm((2, 8, BLK, D), BF16), vm((2, 16, D), F32),
            pltpu.SemaphoreType.DMA((2, 9)), pltpu.SemaphoreType.DMA((2,)),
        ],
        compiler_params=pltpu.CompilerParams(vmem_limit_bytes=63 * 1024 * 1024),
        cost_estimate=pl.CostEstimate(flops=28_000_000_000, bytes_accessed=20_000_000, transcendentals=8_000_000),
    )(count, img, cot, w_all, sp)


PZ = 80
MESH = pl.DeviceIdType.MESH


def place():
    r = lax.axis_index("replica")
    s = lax.axis_index("shard")
    core = lax.rem(r, 2)
    xlo = lax.rem(lax.div(r, 2), 2)
    return dict(x=lax.rem(s, 2) * 2 + xlo, y=lax.div(s, 2), z=lax.div(r, 4), c=core)


def device(p, **change):
    q = dict(p, **change)
    return (q["z"] * 4 + lax.rem(q["x"], 2) * 2 + q["c"], q["y"] * 2 + lax.div(q["x"], 2))


def step_on(p, axis, d):
    return lax.rem(p[axis] + d, 4)


def part(ref, t, x=None, y=None, z=None):
    w = slice(None)
    return ref.at[w if y is None else y, w if x is None else lax.div(x, 2),
                  w if x is None else lax.rem(x, 2), w if z is None else z,
                  :, pl.ds(128 * t, 128)]


class Sender:
    def __init__(self, send, recv):
        self.send, self.recv, self.n, self.out = send, recv, 0, []

    def __call__(self, src, dst, dev):
        cp = pltpu.make_async_remote_copy(src_ref=src, dst_ref=dst, send_sem=self.send.at[self.n],
                                          recv_sem=self.recv.at[self.n], device_id=dev,
                                          device_id_type=MESH)
        self.n += 1
        cp.start()
        self.out.append(cp)
        return cp

    def drain(self):
        for cp in self.out:
            cp.wait_send()


def greet(devs):
    barrier = pltpu.get_barrier_semaphore()
    for dev in devs:
        pl.semaphore_signal(barrier, inc=1, device_id=dev, device_id_type=MESH)
    pl.semaphore_wait(barrier, len(devs))


def fetch_kernel(joint, merge, expand, reduce_w, vec, w, own, send, recv, lsem):
    p = place()
    c, x, y, z = p["c"], p["x"], p["y"], p["z"]
    xhi, xlo = lax.div(x, 2), lax.rem(x, 2)
    partner = device(p, c=1 - c)
    across = device(p, x=3 - x)
    devs = [partner] + [device(p, **{a: step_on(p, a, d)}) for a in "xyz" for d in (1, 2, 3)]
    barrier = pltpu.get_barrier_semaphore()
    for dev in devs:
        pl.semaphore_signal(barrier, inc=1, device_id=dev, device_id_type=MESH)

    blocks = []
    for cb in range(3):
        blocks.append((48 * cb, joint[c, :, pl.ds(D * cb, D)]))
    blocks.append((144, merge[c]))
    for cb in range(4):
        blocks.append((192 + 48 * cb, expand[c, :, pl.ds(D * cb, D)]))
    blocks.append((384, reduce_w[c]))
    blocks.append((576, vec[c]))
    flat = jnp.concatenate([b.astype(BF16) for _, b in blocks]
                           + [jnp.zeros((48, D), BF16)], axis=0)
    own[...] = flat.reshape(2, 4, PZ, D)
    pl.semaphore_wait(barrier, len(devs))

    go = Sender(send, recv)
    wc = w.at[c]

    def mine(t, a=None, b=None):
        s = slice(None)
        return own.at[s if a is None else a, s if b is None else b, :, pl.ds(128 * t, 128)]

    def home(t, a=None, b=None):
        s = slice(None)
        return wc.at[y, xhi, s if a is None else a, s if b is None else b, :, pl.ds(128 * t, 128)]

    local = []
    for t, (a, b) in enumerate([(xlo, None), (None, z), (None, None)]):
        cp = pltpu.make_async_copy(mine(t, a, b), home(t, a, b), lsem.at[t])
        cp.start()
        local.append(cp)
    c1 = go(mine(2), home(2), across)
    a1 = [go(mine(0, xlo, None), home(0, xlo, None), device(p, y=step_on(p, "y", d))) for d in (1, 3, 2)]
    b1 = [go(mine(1, None, z), home(1, None, z), device(p, y=step_on(p, "y", d))) for d in (1, 3, 2)]
    for cp in local:
        cp.wait()
    c1.wait_recv()
    src = part(wc, 2, y=y)
    c2 = [go(src, src, device(p, y=step_on(p, "y", d))) for d in (1, 3, 2)]
    for cp in a1:
        cp.wait_recv()
    src = part(wc, 0, x=x)
    a2 = [go(src, src, device(p, x=step_on(p, "x", d))) for d in (1, 3, 2)]
    for cp in b1:
        cp.wait_recv()
    src = wc.at[:, xhi, :, z, :, pl.ds(128, 128)]
    b2 = go(src, src, across)
    b2.wait_recv()
    src = part(wc, 1, z=z)
    b3 = [go(src, src, device(p, z=step_on(p, "z", d))) for d in (1, 3, 2)]
    last = []
    fw = lambda r: last.append(go(r, r, partner))
    fw(part(wc, 0, x=x))
    fw(part(wc, 1, z=z))
    fw(part(wc, 2, y=y))
    for k, d in enumerate((3, 1, 2)):
        a2[k].wait_recv()
        fw(part(wc, 0, x=step_on(p, "x", d)))
        c2[k].wait_recv()
        fw(part(wc, 2, y=step_on(p, "y", d)))
        b3[k].wait_recv()
        fw(part(wc, 1, z=step_on(p, "z", d)))
    for cp in last:
        cp.wait_recv()
    go.drain()


def fetch(joint, merge, expand, reduce_w, vec):
    V = pl.BlockSpec(memory_space=pltpu.VMEM)
    return pl.pallas_call(
        fetch_kernel,
        out_shape=jax.ShapeDtypeStruct((2, 4, 2, 2, 4, PZ, D), BF16),
        in_specs=[V] * 5,
        out_specs=pl.BlockSpec(memory_space=pl.ANY),
        scratch_shapes=[pltpu.VMEM((2, 4, PZ, D), BF16), pltpu.SemaphoreType.DMA((32,)),
                        pltpu.SemaphoreType.DMA((32,)), pltpu.SemaphoreType.DMA((3,))],
        compiler_params=pltpu.CompilerParams(collective_id=0, has_side_effects=True,
                                             vmem_limit_bytes=32 * 1024 * 1024),
    )(joint, merge, expand, reduce_w, vec)


ORDER = ("xyz", "yzx", "zxy")


def reduce_kernel(g, o, s_buf, cr, ra1, rb1, rc1, ra2, rb2, rc2, ra3, rb3, rc3, o_buf,
                  send, recv, lsem):
    p = place()
    c, x, y, z = p["c"], p["x"], p["y"], p["z"]
    xhi, xlo = lax.div(x, 2), lax.rem(x, 2)
    partner = device(p, c=1 - c)
    devs = [partner] + [device(p, **{a: step_on(p, a, d)}) for a in "xyz" for d in (1, 2, 3)]
    xpair = xhi * 2 + 1 - xlo
    devs += [device(p, x=xpair, z=step_on(p, "z", d)) for d in (1, 2, 3)]
    greet(devs)
    go = Sender(send, recv)
    slots = [[ra1, ra2, ra3], [rb1, rb2, rb3], [rc1, rc2, rc3]]

    swaps, loads = {}, {}
    for n, d in enumerate((1, 3, 2, 0)):
        for t in range(3):
            a = ORDER[t][0]
            at = {a: step_on(p, a, d)}
            swaps[t, d] = go(part(g.at[1 - c], t, **at), part(cr, t, **at), partner)
            cp = pltpu.make_async_copy(part(g.at[c], t, **at), part(s_buf, t, **at),
                                       lsem.at[3 * n + t])
            cp.start()
            loads[t, d] = cp

    def each(t, fixed, body):
        free = [a for a in "yxz" if a not in fixed]
        n = 4 ** len(free)

        def one(i, _):
            at = dict(fixed)
            k = i
            for a in reversed(free):
                at[a] = lax.rem(k, 4)
                k = lax.div(k, 4)
            body(at, free)
            return 0

        if n == 1:
            one(0, 0)
        else:
            lax.fori_loop(0, n, one, 0)

    def spot(at, t):
        return (at["y"], lax.div(at["x"], 2), lax.rem(at["x"], 2), at["z"], slice(None),
                pl.ds(128 * t, 128))

    def slot_index(d, at, free):
        idx = [d - 1]
        for a in free:
            idx += [lax.div(at["x"], 2), lax.rem(at["x"], 2)] if a == "x" else [at[a]]
        return tuple(idx)

    first = {}
    for d in (1, 3, 2, 0):
        for t in range(3):
            a = ORDER[t][0]
            pos = step_on(p, a, d)
            loads[t, d].wait()
            swaps[t, d].wait_recv()

            def merge(at, free, t=t):
                k = spot(at, t)
                s_buf[k] = (s_buf[k].astype(F32) + cr[k].astype(F32)).astype(BF16)

            each(t, {a: pos}, merge)
            if d:
                first[t, d] = go(part(s_buf, t, **{a: pos}), slots[t][0].at[d - 1],
                                 device(p, **{a: pos}))
    held = [dict(), dict(), dict()]
    waiting = first
    for stage in range(3):
        nxt = {}
        for t in range(3):
            a = ORDER[t][stage]
            held[t][a] = p[a]
            for d in (1, 3, 2):
                waiting[t, d].wait_recv()

            def add(at, free, t=t, stage=stage):
                k = spot(at, t)
                v = s_buf[k].astype(F32)
                for d in (1, 2, 3):
                    v = v + slots[t][stage][slot_index(d, at, free)].astype(F32)
                s_buf[k] = v.astype(BF16)

            each(t, held[t], add)
            if stage < 2:
                b = ORDER[t][stage + 1]
                for d in (1, 3, 2):
                    pos = step_on(p, b, d)
                    nxt[t, d] = go(part(s_buf, t, **dict(held[t], **{b: pos})),
                                   slots[t][stage + 1].at[d - 1], device(p, **{b: pos}))
        waiting = nxt

    mine = s_buf.at[y, xhi, xlo, z]
    keep = pltpu.make_async_copy(mine, o_buf.at[c, xlo, z], lsem.at[12])
    keep.start()
    out = []
    for xx in (xpair, x):
        for d in (1, 3, 2, 0):
            if d == 0 and xx is x:
                continue
            out.append(go(mine, o_buf.at[c, xlo, z], device(p, x=xx, z=step_on(p, "z", d))))
    keep.wait()
    for cp in out:
        cp.wait_recv()
    final = go(o_buf.at[c], o_buf.at[c], partner)
    final.wait_recv()
    cp = pltpu.make_async_copy(o_buf, o, lsem.at[13])
    cp.start()
    go.drain()
    cp.wait()


def reduce_grads(g):
    A = pl.BlockSpec(memory_space=pl.ANY)
    vm = lambda *shape: pltpu.VMEM(shape, BF16)
    return pl.pallas_call(
        reduce_kernel,
        out_shape=jax.ShapeDtypeStruct((2, 2, 4, PZ, D), BF16),
        in_specs=[A],
        out_specs=A,
        scratch_shapes=[
            vm(4, 2, 2, 4, PZ, D), vm(4, 2, 2, 4, PZ, D),
            vm(3, 4, 4, PZ, 128), vm(3, 2, 2, 4, PZ, 128), vm(3, 4, 2, 2, PZ, 128),
            vm(3, 4, PZ, 128), vm(3, 2, 2, PZ, 128), vm(3, 4, PZ, 128),
            vm(3, PZ, 128), vm(3, PZ, 128), vm(3, PZ, 128),
            vm(2, 2, 4, PZ, D),
            pltpu.SemaphoreType.DMA((48,)), pltpu.SemaphoreType.DMA((48,)),
            pltpu.SemaphoreType.DMA((14,)),
        ],
        compiler_params=pltpu.CompilerParams(collective_id=1, has_side_effects=True,
                                             vmem_limit_bytes=48 * 1024 * 1024),
    )(g)


BETA_ONE = 0.9
BETA_TWO = 0.999
ADAM_EPS = 1e-08
DECAY_MATRIX = 0.05
RATE_MATRIX = 0.05
RATE_SMALL = 0.4
STEP = 10


def adam_update(gradient, first_moment, second_moment, master, step_rate, decay_rate):
    first_new = BETA_ONE * first_moment + (1.0 - BETA_ONE) * gradient
    second_new = BETA_TWO * second_moment + (1.0 - BETA_TWO) * gradient * gradient
    corrected = first_new / (1.0 - BETA_ONE**STEP)
    denominator = jnp.sqrt(second_new / (1.0 - BETA_TWO**STEP)) + ADAM_EPS
    master_new = master - step_rate * (corrected / denominator + decay_rate * master)
    return (first_new, second_new, master_new)


def adam_kernel(g, *refs):
    ins, outs = refs[:12], refs[12:]
    i = pl.program_id(1)
    for kind, (at, blocks, rows) in enumerate([(0, 3, 16), (144, 1, 16), (192, 4, 16), (384, 1, 64)]):
        step = 48 if rows == 16 else 192
        for cb in range(blocks):
            start = pl.multiple_of(at + step * cb + i * rows, 16)
            grad = g[0, pl.ds(start, rows), :].astype(F32)
            cols = (0, slice(None), pl.ds(D * cb, D))
            m, v, w = (ins[3 * kind + k][cols] for k in range(3))
            new = adam_update(grad, m, v, w, RATE_MATRIX, DECAY_MATRIX)
            for k, val in enumerate((grad,) + new):
                outs[4 * kind + k][cols] = val


def adam(g, firsts, seconds, masters):
    widths = (3 * D, D, 4 * D, D)
    rows = (16, 16, 16, 64)
    spec = [pl.BlockSpec((1, r, w), lambda l, i: (l, i, 0)) for r, w in zip(rows, widths)]
    ins, in_specs, out_specs, shapes = [], [], [], []
    for k in range(4):
        for a in (firsts[k], seconds[k], masters[k]):
            ins.append(a)
            in_specs.append(spec[k])
        for _ in range(4):
            out_specs.append(spec[k])
            shapes.append(jax.ShapeDtypeStruct(masters[k].shape, F32))
    return pl.pallas_call(
        adam_kernel,
        grid=(2, 3),
        out_shape=tuple(shapes),
        in_specs=[pl.BlockSpec((1, BLK, D), lambda l, i: (l, 0, 0))] + in_specs,
        out_specs=tuple(out_specs),
    )(g, *ins)


def shards(images, cotangent, image_count, joint_weight, merge_weight, expand_weight,
           reduce_weight, small_params, joint_first, merge_first, expand_first, reduce_first,
           small_first, joint_second, merge_second, expand_second, reduce_second, small_second):
    masters = (joint_weight, merge_weight, expand_weight, reduce_weight)
    firsts = (joint_first, merge_first, expand_first, reduce_first)
    seconds = (joint_second, merge_second, expand_second, reduce_second)
    width = small_params.shape[1]
    vec = jnp.pad(small_params, ((0, 0), (0, 16 * D - width))).reshape(2, 16, D)
    w = fetch(*masters, vec).reshape(2, 8, BLK, D)
    sp = w[:, :, 576:578].reshape(2, 8, 2 * D)[:, :, :width].reshape(2, 9, D).astype(F32)
    sp = jnp.pad(sp, ((0, 0), (0, 7), (0, 0)))
    block_out, image_grad, g = compute(image_count, images, cotangent, w, sp)
    total = reduce_grads(g.reshape(2, 4, 2, 2, 4, PZ, D)).reshape(2, BLK, D)
    done = adam(total, firsts, seconds, masters)
    rank = lax.axis_index("shard")
    vec_grad = lax.dynamic_slice_in_dim(total[:, 576:585].reshape(2, 9 * D), rank * width, width, 1)
    vec_grad = vec_grad.astype(F32)
    vec_done = (vec_grad,) + adam_update(vec_grad, small_first, small_second, small_params,
                                         RATE_SMALL, 0.0)
    outputs = [block_out, image_grad]
    for member in range(4):
        outputs += [done[4 * kind + member] for kind in range(4)] + [vec_done[member]]
    return tuple(outputs)


def solution(mesh):
    whole = P(("replica", "shard"), None, None)
    weights = [P(None, "shard", None)] * 4 + [P(None, "shard")]
    return jax.shard_map(
        shards,
        mesh=mesh,
        in_specs=(whole, whole, P(("replica", "shard"))) + tuple(weights * 3),
        out_specs=(whole, whole) + tuple(weights * 4),
        check_vma=False,
    )
```

```python
import jax
import jax.numpy as jnp
from jax import lax
from jax.experimental import pallas as pl
from jax.experimental.pallas import tpu as pltpu
from jax.sharding import PartitionSpec as P

D = 384
FF = 1536
HD = 64
NI = 6
SEQ = 197
R = 208
T = NI * R
CH = 416
NCH = T // CH
BLK = 640
JOINT, MERGE, VEC, EXPAND, REDUCE = 0, 144, 192, 256, 448
NORM_EPS = 1e-6
F32 = jnp.float32
BF16 = jnp.bfloat16
MESH = pl.DeviceIdType.MESH
HOPS = (1, 3, 2)


def dot(a, b):
    return lax.dot_general(a, b, (((1,), (0,)), ((), ())), preferred_element_type=F32)


def dot_nt(a, b):
    return lax.dot_general(a, b, (((1,), (1,)), ((), ())), preferred_element_type=F32)


def dot_tn(a, b):
    return lax.dot_general(a, b, (((0,), (0,)), ((), ())), preferred_element_type=F32)


def normalize(v):
    centered = v - jnp.mean(v, axis=-1, keepdims=True)
    variance = jnp.mean(centered * centered, axis=-1, keepdims=True)
    rstd = lax.rsqrt(variance + NORM_EPS)
    return centered * rstd, rstd


def gelu_pair(u):
    z = jnp.abs(u)
    d = 1.0 + (0.3275911 * 0.7071067811865476) * z
    t = 1.0 / d
    e = jnp.exp(-0.5 * (u * u))
    poly = ((((0.5 * 1.061405429) * t - 0.5 * 1.453152027) * t + 0.5 * 1.421413741) * t
            - 0.5 * 0.284496736) * t + 0.5 * 0.254829592
    half = poly * t * e
    phi = jnp.where(u < 0, half, 1.0 - half)
    return u * phi, phi + u * (e * 0.3989422804014327)


def norm_back(dy, xhat, rstd, gain):
    dxh = dy * gain
    m1 = jnp.mean(dxh, axis=-1, keepdims=True)
    m2 = jnp.mean(dxh * xhat, axis=-1, keepdims=True)
    return rstd * (dxh - m1 - xhat * m2)


class Place:
    def __init__(self):
        r = lax.axis_index("replica")
        s = lax.axis_index("shard")
        self.c = lax.rem(r, 2)
        self.xlo = lax.rem(lax.div(r, 2), 2)
        self.z = lax.div(r, 4)
        self.xhi = lax.rem(s, 2)
        self.y = lax.div(s, 2)
        self.x = self.xhi * 2 + self.xlo
        self.twin = self.xhi * 2 + 1 - self.xlo

    def at(self, **change):
        q = dict(x=self.x, y=self.y, z=self.z, c=self.c, **{})
        q.update(change)
        return (q["z"] * 4 + lax.rem(q["x"], 2) * 2 + q["c"], q["y"] * 2 + lax.div(q["x"], 2))

    def step(self, axis, d):
        return lax.rem(getattr(self, axis) + d, 4)

    def partner(self):
        return self.at(c=1 - self.c)

    def across(self):
        return self.at(x=3 - self.x)


def lanes(t):
    return pl.ds(128 * t, 128)


def span(start, n):
    return pl.ds(pl.multiple_of(start, 16), n)


class Group:
    def __init__(self, p, l, g0, n):
        self.p, self.l, self.g0, self.n, self.h = p, l, g0, n, n // 2

    def a_rows(self, xlo, c=None):
        return span(self.base(c) + xlo * (self.n // 4), self.n // 4)

    def b_rows(self, z, c=None):
        return span(self.base(c) + z * (self.n // 8), self.n // 8)

    def c_rows(self, c=None):
        return span(self.base(c), self.h)

    def base(self, c=None):
        return self.g0 + (self.p.c if c is None else c) * self.h


class Messages:
    def __init__(self, send, recv):
        self.send, self.recv, self.n, self.made = send, recv, 0, []

    def new(self, src, dst, dev):
        k = self.n
        self.n += 1

        def build():
            return pltpu.make_async_remote_copy(
                src_ref=src(), dst_ref=dst(), send_sem=self.send.at[k], recv_sem=self.recv.at[k],
                device_id=dev(), device_id_type=MESH)

        self.made.append(build)
        return build


def start(*groups):
    for group in groups:
        for build in group:
            build().start()


def arrive(*groups):
    for group in groups:
        for build in group:
            build().wait_recv()


class Fetch:
    def __init__(self, p, g, msgs, w, own):
        self.g = g
        wl, ol = w.at[g.l], own.at[g.l]
        s = slice(None)
        ra, rb, rc = (lambda v=None: g.a_rows(p.xlo if v is None else v),
                      lambda v=None: g.b_rows(p.z if v is None else v), lambda: g.c_rows())
        oa = lambda: ol.at[ra(), lanes(0)]
        ob = lambda: ol.at[rb(), lanes(1)]
        oc = lambda: ol.at[rc(), lanes(2)]
        ha = lambda: wl.at[p.y, p.xhi, ra(), lanes(0)]
        hb = lambda: wl.at[p.y, p.xhi, rb(), lanes(1)]
        hc = lambda: wl.at[p.y, p.xhi, rc(), lanes(2)]
        self.local = [(oa, ha), (ob, hb), (oc, hc)]
        ydev = lambda d: (lambda: p.at(y=p.step("y", d)))
        xdev = lambda d: (lambda: p.at(x=p.step("x", d)))
        zdev = lambda d: (lambda: p.at(z=p.step("z", d)))
        self.c1 = [msgs.new(oc, hc, p.across)]
        self.a1 = [msgs.new(oa, ha, ydev(d)) for d in HOPS]
        self.b1 = [msgs.new(ob, hb, ydev(d)) for d in HOPS]
        ax = lambda x: (lambda: wl.at[s, lax.div(x(), 2), ra(lax.rem(x(), 2)), lanes(0)])
        cy = lambda y: (lambda: wl.at[y(), s, rc(), lanes(2)])
        bz = lambda z: (lambda: wl.at[s, s, rb(z()), lanes(1)])
        bx = lambda: wl.at[s, p.xhi, rb(), lanes(1)]
        x0, y0, z0 = (lambda: p.x), (lambda: p.y), (lambda: p.z)
        self.a2 = [msgs.new(ax(x0), ax(x0), xdev(d)) for d in HOPS]
        self.c2 = [msgs.new(cy(y0), cy(y0), ydev(d)) for d in HOPS]
        self.b2 = [msgs.new(bx, bx, p.across)]
        self.b3 = [msgs.new(bz(z0), bz(z0), zdev(d)) for d in HOPS]
        fw = lambda r: msgs.new(r, r, p.partner)
        back = lambda axis, d: (lambda: p.step(axis, (4 - d) % 4))
        self.fa = [fw(ax(back("x", d))) for d in (0,) + HOPS]
        self.fb = [fw(bz(back("z", d))) for d in (0,) + HOPS]
        self.fc = [fw(cy(back("y", d))) for d in (0,) + HOPS]

    def s1(self, lsem):
        start(self.c1, self.a1, self.b1)
        copies = [pltpu.make_async_copy(a(), b(), lsem.at[k]) for k, (a, b) in enumerate(self.local)]
        for cp in copies:
            cp.start()
        for cp in copies:
            cp.wait()

    def s2(self):
        arrive(self.c1)
        start(self.c2)
        arrive(self.b1)
        start(self.b2)
        arrive(self.a1)
        start(self.a2, self.fa[:1])

    def s3(self):
        arrive(self.b2)
        start(self.b3, self.fb[:1], self.fc[:1])

    def s4(self):
        for k in range(3):
            for got, pass_on in ((self.c2, self.fc), (self.a2, self.fa), (self.b3, self.fb)):
                arrive(got[k:k + 1])
                start(pass_on[k + 1:k + 2])

    def done(self):
        arrive(self.fa, self.fb, self.fc)


class Reduce:
    def __init__(self, p, g, msgs, grad, total, cr, a, b, c):
        self.p, self.g = p, g
        s = slice(None)
        n4, n8, h = g.n // 4, g.n // 8, g.h
        gl = grad.at[g.l]
        tl = total.at[g.l]
        self.gl_ref, self.tl, self.cr = gl, tl, cr
        self.a, self.b, self.c = a, b, c
        hi, lo = (lambda v: lax.div(v, 2)), (lambda v: lax.rem(v, 2))
        go = lambda axis, d: (lambda: p.step(axis, d))
        dev = lambda axis, d: (lambda: p.at(**{axis: p.step(axis, d)}))
        other = lambda: 1 - p.c
        self.swap = {}
        for d in HOPS + (0,):
            x, y, z = go("x", d), go("y", d), go("z", d)
            self.swap[0, d] = msgs.new(
                lambda x=x: gl.at[s, hi(x()), g.a_rows(lo(x()), other()), lanes(0)],
                lambda x=x: cr.at[s, hi(x()), span(lo(x()) * n4, n4), lanes(0)], p.partner)
            self.swap[1, d] = msgs.new(
                lambda z=z: gl.at[s, s, g.b_rows(z(), other()), lanes(1)],
                lambda z=z: cr.at[s, s, span(z() * n8, n8), lanes(1)], p.partner)
            self.swap[2, d] = msgs.new(
                lambda y=y: gl.at[y(), s, g.c_rows(other()), lanes(2)],
                lambda y=y: cr.at[y(), s, pl.ds(0, h), lanes(2)], p.partner)
        self.first = {}
        for d in HOPS:
            x, y, z = go("x", d), go("y", d), go("z", d)
            self.first[0, d] = msgs.new(
                lambda x=x: gl.at[s, hi(x()), g.a_rows(lo(x())), lanes(0)],
                lambda d=d: a[0].at[d - 1], dev("x", d))
            self.first[1, d] = msgs.new(
                lambda z=z: gl.at[s, s, g.b_rows(z()), lanes(1)],
                lambda d=d: b[0].at[d - 1], dev("z", d))
            self.first[2, d] = msgs.new(
                lambda y=y: gl.at[y(), s, g.c_rows(), lanes(2)],
                lambda d=d: c[0].at[d - 1], dev("y", d))
        self.second = []
        self.third = []
        self.share = []
        for d in HOPS:
            x, y = go("x", d), go("y", d)
            self.second.append(msgs.new(
                lambda y=y: gl.at[y(), p.xhi, g.a_rows(p.xlo), lanes(0)],
                lambda d=d: a[1].at[d - 1], dev("y", d)))
            self.second.append(msgs.new(
                lambda y=y: gl.at[y(), s, g.b_rows(p.z), lanes(1)],
                lambda d=d: b[1].at[d - 1], dev("y", d)))
            self.second.append(msgs.new(
                lambda x=x: gl.at[p.y, hi(x()), g.c_rows(), lanes(2)],
                lambda: c[1].at[p.x], dev("x", d)))
            self.third.append(msgs.new(lambda: a[2].at[p.z], lambda: a[2].at[p.z], dev("z", d)))
            self.third.append(msgs.new(lambda x=x: b[2].at[hi(x())], lambda: b[3].at[p.x], dev("x", d)))
            self.third.append(msgs.new(lambda: c[2].at[p.z], lambda: c[2].at[p.z], dev("z", d)))
            rb = lambda: tl.at[g.b_rows(p.z), lanes(1)]
            self.share.append(msgs.new(rb, rb, dev("z", d)))
        ra = lambda: tl.at[g.a_rows(p.xlo), lanes(0)]
        self.share.append(msgs.new(ra, ra, lambda: p.at(x=p.twin)))
        rc = lambda: tl.at[g.c_rows(), :]
        self.final = [msgs.new(rc, rc, p.partner)]

    def begin(self):
        for d in HOPS + (0,):
            start([self.swap[t, d] for t in range(3)])

    def s1(self):
        p, g, grad, cr, l = self.p, self.g, self.gl_ref, self.cr, self.g.l
        n4, n8, h = g.n // 4, g.n // 8, g.h

        def add(gi, ci):
            grad[gi] = (grad[gi].astype(F32) + cr[ci].astype(F32)).astype(BF16)

        for d in HOPS + (0,):
            x, y, z = p.step("x", d), p.step("y", d), p.step("z", d)
            arrive([self.swap[0, d]])

            @pl.loop(0, 4)
            def _(k):
                add((k, lax.div(x, 2), g.a_rows(lax.rem(x, 2)), lanes(0)),
                    (k, lax.div(x, 2), span(lax.rem(x, 2) * n4, n4), lanes(0)))

            if d:
                start([self.first[0, d]])
            arrive([self.swap[1, d]])

            @pl.loop(0, 4)
            def _(k):
                for j in range(2):
                    add((k, j, g.b_rows(z), lanes(1)), (k, j, span(z * n8, n8), lanes(1)))

            if d:
                start([self.first[1, d]])
            arrive([self.swap[2, d]])

            @pl.loop(0, 2)
            def _(k):
                add((y, k, g.c_rows(), lanes(2)), (y, k, pl.ds(0, h), lanes(2)))

            if d:
                start([self.first[2, d]])

    def s2(self):
        p, g, grad, l = self.p, self.g, self.gl_ref, self.g.l
        arrive([self.first[0, d] for d in HOPS])

        def add(gi, ref, tail):
            v = grad[gi].astype(F32)
            for k in range(3):
                v = v + ref[(k,) + tail].astype(F32)
            grad[gi] = v.astype(BF16)

        @pl.loop(0, 4)
        def _(k):
            add((k, p.xhi, g.a_rows(p.xlo), lanes(0)), self.a[0], (k,))

        start(self.second[0::3])
        arrive([self.first[1, d] for d in HOPS])

        @pl.loop(0, 4)
        def _(k):
            for j in range(2):
                add((k, j, g.b_rows(p.z), lanes(1)), self.b[0], (k, j))

        start(self.second[1::3])
        arrive([self.first[2, d] for d in HOPS])

        @pl.loop(0, 2)
        def _(k):
            add((p.y, k, g.c_rows(), lanes(2)), self.c[0], (k,))

        start(self.second[2::3])
        self.c[1][p.x] = grad[p.y, p.xhi, g.c_rows(), lanes(2)]

    def s3(self):
        p, g, grad = self.p, self.g, self.gl_ref
        arrive(self.second[0::3])
        v = grad[p.y, p.xhi, g.a_rows(p.xlo), lanes(0)].astype(F32)
        for k in range(3):
            v = v + self.a[1][k].astype(F32)
        self.a[2][p.z] = v.astype(BF16)
        start(self.third[0::3])
        arrive(self.second[1::3])
        for j in range(2):
            v = grad[p.y, j, g.b_rows(p.z), lanes(1)].astype(F32)
            for k in range(3):
                v = v + self.b[1][k, j].astype(F32)
            self.b[2][j] = v.astype(BF16)
        start(self.third[1::3])
        self.b[3][p.x] = self.b[2][p.xhi]
        arrive(self.second[2::3])
        v = self.c[1][0].astype(F32)
        for k in range(1, 4):
            v = v + self.c[1][k].astype(F32)
        self.c[2][p.z] = v.astype(BF16)
        start(self.third[2::3])

    def s4(self):
        p, g, tl = self.p, self.g, self.tl

        def total(ref):
            v = ref[0].astype(F32)
            for k in range(1, 4):
                v = v + ref[k].astype(F32)
            return v.astype(BF16)

        arrive(self.third[0::3])
        tl[g.a_rows(p.xlo), lanes(0)] = total(self.a[2])
        start(self.share[3:])
        arrive(self.third[1::3])
        tl[g.b_rows(p.z), lanes(1)] = total(self.b[3])
        start(self.share[:3])
        arrive(self.third[2::3])
        tl[g.c_rows(), lanes(2)] = total(self.c[2])

    def s5(self):
        arrive(self.share)
        start(self.final)

    def done(self):
        arrive(self.final)


FFN_ROWS = (EXPAND, 384)
ATT_ROWS = (0, 256)
N_COMM = 12


def train_kernel(count, img, cot, joint, merge, expand, reduce_w, vec_in,
                 out, dimg, total_out, g_spill, gp_spill,
                 w, own, sp, xs, hs, a_s, c_s, o_s, qkv, g_s, gp_s, dx_s, dzb_s, dyb_s, dob_s,
                 lse_s, grad, small, total, in_stage, out_stage, *rest):
    slots, (send, recv, lsem, wsem) = rest[:4 * N_COMM], rest[4 * N_COMM:]
    p = Place()
    barrier = pltpu.get_barrier_semaphore()
    friends = [p.partner()] + [p.at(**{a: p.step(a, d)}) for a in "xyz" for d in HOPS]
    for dev in friends:
        pl.semaphore_signal(barrier, inc=1, device_id=dev, device_id_type=MESH)

    msgs = Messages(send, recv)
    F = [[Fetch(p, Group(p, l, *rows), msgs, w, own) for rows in (ATT_ROWS, FFN_ROWS)] for l in range(2)]
    RD = {}
    for n, (l, rows) in enumerate([(1, FFN_ROWS), (1, ATT_ROWS), (0, FFN_ROWS), (0, ATT_ROWS)]):
        q = slots[N_COMM * n:N_COMM * (n + 1)]
        RD[l, rows] = Reduce(p, Group(p, l, *rows), msgs, grad, total, q[0], q[1:4], q[4:8], q[8:11])

    pieces = []
    for l in range(2):
        for cb in range(3):
            pieces.append((l, joint.at[l, :, pl.ds(D * cb, D)], JOINT + 48 * cb, 48))
        pieces.append((l, merge.at[l], MERGE, 48))
        pieces.append((l, vec_in.at[l], VEC, 16))
        for cb in range(4):
            pieces.append((l, expand.at[l, :, pl.ds(D * cb, D)], EXPAND + 48 * cb, 48))
        pieces.append((l, reduce_w.at[l], REDUCE, 192))
    loads = [pltpu.make_async_copy(src, hs.at[l, pl.ds(at, n), :], wsem.at[k])
             for k, (l, src, at, n) in enumerate(pieces)]
    for cp in loads:
        cp.start()
    get_img = pltpu.make_async_copy(img, in_stage, lsem.at[3])
    get_img.start()
    for k, cp in enumerate(loads):
        cp.wait()
        if k % 10 == 9:
            l = k // 10
            own[l, 0:VEC + 16, :] = hs[l, 0:VEC + 16, :].astype(BF16)
            own[l, EXPAND:BLK, :] = hs[l, EXPAND:BLK, :].astype(BF16)
    pl.semaphore_wait(barrier, len(friends))

    f = F[0][0]
    f.s1(lsem)

    n_live = count[0]

    def rows_of(c):
        return pl.ds(pl.multiple_of(c * CH, CH), CH)

    def img_rows(i, n=R):
        return pl.ds(pl.multiple_of(i * R, R), n)

    def tail_rows(i):
        return pl.ds(pl.multiple_of(i * R, R) + 192, 16)

    get_img.wait()

    @pl.loop(0, NI)
    def _(i):
        xs[0, tail_rows(i), :] = jnp.zeros((16, D), F32)
        xs[0, img_rows(i, SEQ), :] = in_stage[i].astype(F32)

    get_cot = pltpu.make_async_copy(cot, in_stage, lsem.at[3])
    get_cot.start()
    f.s2()
    f.s3()
    f.s4()
    f.done()

    lane = lax.broadcasted_iota(jnp.int32, (R, 128), 1)
    key_ok = lax.broadcasted_iota(jnp.int32, (R, R), 0) < SEQ

    def half(v, e):
        keep = (lane < HD) if e == 0 else (lane >= HD)
        return jnp.where(keep, v, jnp.zeros_like(v))

    def weight(l, at):
        return w[l, :, :, pl.ds(at, 48), :].reshape(D, D)

    def reduce_rows(l, k):
        return w[l, k, :, pl.ds(REDUCE, 192), :].reshape(D, D)

    plan = {}

    def during(phase, l, step, *calls):
        plan.setdefault((phase, l), {}).setdefault(step, []).extend(calls)

    def run(phase, l, n, body):
        at = plan.get((phase, l), {})

        def one(i, _):
            for step, calls in at.items():
                @pl.when(i == step)
                def _():
                    for call in calls:
                        call()
            body(i)
            return 0

        lax.fori_loop(0, n, one, 0)

    during("p1", 0, 0, lambda: F[0][1].s1(lsem))
    during("p2", 0, 0, F[0][1].s2)
    during("p2", 0, 2, F[0][1].s3)
    during("p2", 0, 3, lambda: F[1][0].s1(lsem))
    during("p2", 0, 4, F[0][1].s4)
    during("p2", 0, 5, F[1][0].s2)
    during("p3", 0, 0, F[1][0].s3)
    during("p3", 0, 1, F[1][0].s4, lambda: F[1][1].s1(lsem))
    during("p3", 0, 2, F[1][1].s2)
    during("p1", 1, 0, F[1][1].s3)
    during("p2", 1, 2, F[1][1].s4)

    spills = [(g_s, g_spill, lsem.at[4]), (gp_s, gp_spill, lsem.at[5])]

    for l in range(2):
        if l:
            F[1][0].done()
        acc = w[l, 0, 0, pl.ds(VEC, 16), :].astype(F32)
        for s in range(1, 8):
            acc = acc + w[l, s // 2, s % 2, pl.ds(VEC, 16), :].astype(F32)
        sp[l] = acc
        vec = lambda r: sp[l, r:r + 1, :]

        def p1(c):
            rows = rows_of(c)
            xhat, _r = normalize(xs[l, rows, :])
            a = (xhat * vec(0) + vec(1)).astype(BF16)
            a_s[l, rows, :] = a
            for cb in range(3):
                part = dot(a, weight(l, JOINT + 48 * cb))
                if cb == 0:
                    part = part * (HD ** -0.5)
                qkv[l, rows, pl.ds(D * cb, D)] = part.astype(BF16)

        run("p1", l, NCH, p1)

        def p2(i):
            rows = img_rows(i)
            for j in range(3):
                q2 = qkv[l, rows, pl.ds(128 * j, 128)]
                k2 = qkv[l, rows, pl.ds(D + 128 * j, 128)]
                v2 = qkv[l, rows, pl.ds(2 * D + 128 * j, 128)]
                v2t = v2.T
                parts = []
                for e in range(2):
                    st = dot_nt(k2, half(q2, e))
                    st = jnp.where(key_ok, st, -1e30)
                    m = jnp.max(st, axis=0, keepdims=True)
                    pt = jnp.exp(st - m)
                    tot = jnp.sum(pt, axis=0, keepdims=True)
                    pbt = (pt * (1.0 / tot)).astype(BF16)
                    lse_s[l, i, 2 * j + e:2 * j + e + 1, :] = m + jnp.log(tot)
                    parts.append(dot(v2t[HD * e:HD * (e + 1), :], pbt))
                o_s[l, rows, pl.ds(128 * j, 128)] = jnp.concatenate(parts, axis=0).T.astype(BF16)

        run("p2", l, NI, p2)

        F[l][1].done()
        if l:
            for src, dst, sem in spills:
                pltpu.make_async_copy(src, dst, sem).wait()

        def p3(c):
            rows = rows_of(c)
            h = xs[l, rows, :] + dot(o_s[l, rows, :], weight(l, MERGE))
            hs[l, rows, :] = h
            xhat, _r = normalize(h)
            cc = (xhat * vec(2) + vec(3)).astype(BF16)
            c_s[l, rows, :] = cc
            acc = h + vec(4)
            for f in range(4):
                u = dot(cc, weight(l, EXPAND + 48 * f)) + vec(5 + f)
                g, gp = gelu_pair(u)
                g = g.astype(BF16)
                g_s[rows, pl.ds(D * f, D)] = g
                gp_s[rows, pl.ds(D * f, D)] = gp.astype(BF16)
                acc = acc + dot(g, reduce_rows(l, f))
            if l == 0:
                xs[1, rows, :] = acc
            else:
                for k in range(CH // R):
                    i = c * (CH // R) + k
                    live = jnp.where(i < n_live, 1.0, 0.0).astype(F32)
                    out_stage[i] = acc[R * k:R * k + SEQ, :] * live

        run("p3", l, NCH, p3)
        if l == 0:
            for src, dst, sem in spills:
                pltpu.make_async_copy(src, dst, sem).start()

    put_out = pltpu.make_async_copy(out_stage, out, lsem.at[6])
    put_out.start()
    small[...] = jnp.zeros_like(small)
    get_cot.wait()

    @pl.loop(0, NI)
    def _(i):
        live = jnp.where(i < n_live, 1.0, 0.0).astype(F32)
        dx_s[tail_rows(i), :] = jnp.zeros((16, D), F32)
        dx_s[img_rows(i, SEQ), :] = in_stage[i].astype(F32) * live

    R1, R2, R3, R4 = RD[1, FFN_ROWS], RD[1, ATT_ROWS], RD[0, FFN_ROWS], RD[0, ATT_ROWS]
    during("b2", 1, 1, R1.s1)
    during("b2", 1, 4, R1.s2)
    during("b3", 1, 0, R1.s3)
    during("b1", 0, 0, R1.s4)
    during("b1", 0, 1, R2.s1, R1.s5)
    during("b2", 0, 0, R2.s2)
    during("b2", 0, 1, R3.s1)
    during("b2", 0, 2, R2.s3)
    during("b2", 0, 4, R2.s4, R3.s2)
    during("b3", 0, 0, R2.s5, R3.s3)
    during("b3", 0, 2, R3.s4)

    def colsum(v):
        return jnp.sum(v, axis=0, keepdims=True)

    for l in (1, 0):
        vec = lambda r: sp[l, r:r + 1, :]
        if l == 0:
            for dst, src, sem in spills:
                pltpu.make_async_copy(src, dst, sem).wait()

        def b1(c):
            rows = rows_of(c)
            dx = dx_s[rows, :]
            dzb = dx.astype(BF16)
            dzb_s[rows, :] = dzb
            small[l, 4:5, :] += colsum(dzb.astype(F32))
            dc = None
            for f in range(4):
                dg = dot_nt(dzb, reduce_rows(l, f))
                du = (dg * gp_s[rows, pl.ds(D * f, D)].astype(F32)).astype(BF16)
                gp_s[rows, pl.ds(D * f, D)] = du
                small[l, 5 + f:6 + f, :] += colsum(du.astype(F32))
                part = dot_nt(du, weight(l, EXPAND + 48 * f))
                dc = part if dc is None else dc + part
            xhat, rstd = normalize(hs[l, rows, :])
            small[l, 2:3, :] += colsum(dc * xhat)
            small[l, 3:4, :] += colsum(dc)
            dh = dx + norm_back(dc, xhat, rstd, vec(2))
            dx_s[rows, :] = dh
            dyb = dh.astype(BF16)
            dyb_s[rows, :] = dyb
            dob_s[rows, :] = dot_nt(dyb, weight(l, MERGE)).astype(BF16)

        run("b1", l, NCH, b1)

        def shard_store(at, val):
            grad[l, :, :, pl.ds(at, 48), :] = val.astype(BF16).reshape(4, 2, 48, D)

        for f in range(4):
            shard_store(EXPAND + 48 * f, dot_tn(c_s[l], gp_s[:, pl.ds(D * f, D)]))
        for f in range(4):
            val = dot_tn(dzb_s[...], g_s[:, pl.ds(D * f, D)])
            grad[l, f, :, pl.ds(REDUCE, 192), :] = val.T.astype(BF16).reshape(2, 192, D)
        RD[l, FFN_ROWS].begin()
        if l:
            for dst, src, sem in spills:
                pltpu.make_async_copy(src, dst, sem).start()
        shard_store(MERGE, dot_tn(o_s[l], dyb_s[...]))

        def b2(i):
            rows = img_rows(i)
            for j in range(3):
                q2 = qkv[l, rows, pl.ds(128 * j, 128)]
                k2 = qkv[l, rows, pl.ds(D + 128 * j, 128)]
                v2 = qkv[l, rows, pl.ds(2 * D + 128 * j, 128)]
                do2 = dob_s[rows, pl.ds(128 * j, 128)]
                k2t = k2.T
                dv = dk = None
                dqt = []
                for e in range(2):
                    qe = half(q2, e)
                    de = half(do2, e)
                    st = dot_nt(k2, qe)
                    pt = jnp.where(key_ok, jnp.exp(st - lse_s[l, i, 2 * j + e:2 * j + e + 1, :]), 0.0)
                    dpt = dot_nt(v2, de)
                    r = jnp.sum(dpt * pt, axis=0, keepdims=True)
                    dst = (pt * (dpt - r)).astype(BF16)
                    dve = dot(pt.astype(BF16), de)
                    dke = dot(dst, qe)
                    dv = dve if dv is None else dv + dve
                    dk = dke if dk is None else dk + dke
                    dqt.append(dot(k2t[HD * e:HD * (e + 1), :], dst))
                dq = jnp.concatenate(dqt, axis=0).T * (HD ** -0.5)
                qkv[l, rows, pl.ds(128 * j, 128)] = dq.astype(BF16)
                qkv[l, rows, pl.ds(D + 128 * j, 128)] = dk.astype(BF16)
                qkv[l, rows, pl.ds(2 * D + 128 * j, 128)] = dv.astype(BF16)

        run("b2", l, NI, b2)

        if l == 0:
            put_out.wait()

        def b3(c):
            rows = rows_of(c)
            da = None
            for cb in range(3):
                part = dot_nt(qkv[l, rows, pl.ds(D * cb, D)], weight(l, JOINT + 48 * cb))
                da = part if da is None else da + part
            xhat, rstd = normalize(xs[l, rows, :])
            small[l, 0:1, :] += colsum(da * xhat)
            small[l, 1:2, :] += colsum(da)
            dx = dx_s[rows, :] + norm_back(da, xhat, rstd, vec(0))
            if l == 1:
                dx_s[rows, :] = dx
            else:
                for k in range(CH // R):
                    out_stage[c * (CH // R) + k] = dx[R * k:R * k + SEQ, :]

        run("b3", l, NCH, b3)

        for s in range(8):
            grad[l, s // 2, s % 2, pl.ds(VEC, 16), :] = small[l].astype(BF16)
        for cb in range(3):
            shard_store(JOINT + 48 * cb, dot_tn(a_s[l], qkv[l, :, pl.ds(D * cb, D)]))
        RD[l, ATT_ROWS].begin()

    put_grad = pltpu.make_async_copy(out_stage, dimg, lsem.at[6])
    put_grad.start()
    R3.s5()
    R4.s1()
    R4.s2()
    R4.s3()
    R4.s4()
    R4.s5()
    for rd in (R1, R2, R3, R4):
        rd.done()
    put_total = pltpu.make_async_copy(total, total_out, lsem.at[7])
    put_total.start()
    for build in msgs.made:
        build().wait_send()
    put_grad.wait()
    put_total.wait()


def train(count, img, cot, joint, merge, expand, reduce_w, vec):
    A = pl.BlockSpec(memory_space=pl.ANY)
    vm = lambda *shape: pltpu.VMEM(shape, BF16)
    vf = lambda *shape: pltpu.VMEM(shape, F32)
    slots = []
    for n in (384, 256, 384, 256):
        n4, n8, h = n // 4, n // 8, n // 2
        slots += [vm(4, 2, h, D),
                  vm(3, 4, n4, 128), vm(3, n4, 128), vm(4, n4, 128),
                  vm(3, 4, 2, n8, 128), vm(3, 2, n8, 128), vm(2, n8, 128), vm(4, n8, 128),
                  vm(3, 2, h, 128), vm(4, h, 128), vm(4, h, 128), vm(16, 128)]
    return pl.pallas_call(
        train_kernel,
        out_shape=(
            jax.ShapeDtypeStruct((NI, SEQ, D), F32),
            jax.ShapeDtypeStruct((NI, SEQ, D), F32),
            jax.ShapeDtypeStruct((2, BLK, D), BF16),
            jax.ShapeDtypeStruct((T, FF), BF16),
            jax.ShapeDtypeStruct((T, FF), BF16),
        ),
        in_specs=[pl.BlockSpec(memory_space=pltpu.SMEM)] + [A] * 7,
        out_specs=(A,) * 5,
        scratch_shapes=[
            vm(2, 4, 2, BLK, D), vm(2, BLK, D), vf(2, 16, D),
            vf(2, T, D), vf(2, T, D),
            vm(2, T, D), vm(2, T, D), vm(2, T, D),
            vm(2, T, 3 * D), vm(T, FF), vm(T, FF),
            vf(T, D), vm(T, D), vm(T, D), vm(T, D),
            vf(2, NI, 8, R),
            vm(2, 4, 2, BLK, D), vf(2, 16, D), vm(2, BLK, D),
            vm(NI, SEQ, D), vf(NI, SEQ, D),
            *slots,
            pltpu.SemaphoreType.DMA((N_SEMS,)), pltpu.SemaphoreType.DMA((N_SEMS,)),
            pltpu.SemaphoreType.DMA((8,)), pltpu.SemaphoreType.DMA((20,)),
        ],
        compiler_params=pltpu.CompilerParams(collective_id=0, has_side_effects=True,
                                             vmem_limit_bytes=65200 * 1024),
        cost_estimate=pl.CostEstimate(flops=28_000_000_000, bytes_accessed=20_000_000,
                                      transcendentals=8_000_000),
    )(count, img, cot, joint, merge, expand, reduce_w, vec)


N_SEMS = 4 * 29 + 4 * 44


BETA_ONE = 0.9
BETA_TWO = 0.999
ADAM_EPS = 1e-08
DECAY_MATRIX = 0.05
RATE_MATRIX = 0.05
RATE_SMALL = 0.4
STEP = 10


def adam_update(gradient, first_moment, second_moment, master, step_rate, decay_rate):
    first_new = BETA_ONE * first_moment + (1.0 - BETA_ONE) * gradient
    second_new = BETA_TWO * second_moment + (1.0 - BETA_TWO) * gradient * gradient
    corrected = first_new / (1.0 - BETA_ONE**STEP)
    denominator = jnp.sqrt(second_new / (1.0 - BETA_TWO**STEP)) + ADAM_EPS
    master_new = master - step_rate * (corrected / denominator + decay_rate * master)
    return (first_new, second_new, master_new)


def adam_kernel(g, *refs):
    ins, outs = refs[:12], refs[12:]
    i = pl.program_id(1)
    for kind, (at, blocks, rows) in enumerate([(JOINT, 3, 16), (MERGE, 1, 16), (EXPAND, 4, 16), (REDUCE, 1, 64)]):
        for cb in range(blocks):
            start_row = pl.multiple_of(at + 48 * cb + i * rows, 16)
            grad = g[0, pl.ds(start_row, rows), :].astype(F32)
            cols = (0, slice(None), pl.ds(D * cb, D))
            m, v, wt = (ins[3 * kind + k][cols] for k in range(3))
            new = adam_update(grad, m, v, wt, RATE_MATRIX, DECAY_MATRIX)
            for k, val in enumerate((grad,) + new):
                outs[4 * kind + k][cols] = val


def adam(g, firsts, seconds, masters):
    widths = (3 * D, D, 4 * D, D)
    rows = (16, 16, 16, 64)
    spec = [pl.BlockSpec((1, r, wd), lambda l, i: (l, i, 0)) for r, wd in zip(rows, widths)]
    ins, in_specs, out_specs, shapes = [], [], [], []
    for k in range(4):
        for a in (firsts[k], seconds[k], masters[k]):
            ins.append(a)
            in_specs.append(spec[k])
        for _ in range(4):
            out_specs.append(spec[k])
            shapes.append(jax.ShapeDtypeStruct(masters[k].shape, F32))
    return pl.pallas_call(
        adam_kernel,
        grid=(2, 3),
        out_shape=tuple(shapes),
        in_specs=[pl.BlockSpec((1, BLK, D), lambda l, i: (l, 0, 0))] + in_specs,
        out_specs=tuple(out_specs),
    )(g, *ins)


def shards(images, cotangent, image_count, joint_weight, merge_weight, expand_weight,
           reduce_weight, small_params, joint_first, merge_first, expand_first, reduce_first,
           small_first, joint_second, merge_second, expand_second, reduce_second, small_second):
    masters = (joint_weight, merge_weight, expand_weight, reduce_weight)
    firsts = (joint_first, merge_first, expand_first, reduce_first)
    seconds = (joint_second, merge_second, expand_second, reduce_second)
    width = small_params.shape[1]
    rank = lax.axis_index("shard")
    vec = lax.dynamic_update_slice_in_dim(jnp.zeros((2, 16 * D), F32), small_params, rank * width, 1)
    block_out, image_grad, total, _g, _gp = train(
        image_count, images, cotangent, *masters, vec.reshape(2, 16, D))
    done = adam(total, firsts, seconds, masters)
    vec_grad = lax.dynamic_slice_in_dim(total[:, VEC:VEC + 9].reshape(2, 9 * D), rank * width, width, 1)
    vec_grad = vec_grad.astype(F32)
    vec_done = (vec_grad,) + adam_update(vec_grad, small_first, small_second, small_params,
                                         RATE_SMALL, 0.0)
    outputs = [block_out, image_grad]
    for member in range(4):
        outputs += [done[4 * kind + member] for kind in range(4)] + [vec_done[member]]
    return tuple(outputs)


def solution(mesh):
    whole = P(("replica", "shard"), None, None)
    weights = [P(None, "shard", None)] * 4 + [P(None, "shard")]
    return jax.shard_map(
        shards,
        mesh=mesh,
        in_specs=(whole, whole, P(("replica", "shard"))) + tuple(weights * 3),
        out_specs=(whole, whole) + tuple(weights * 4),
        check_vma=False,
    )
```

```python
import jax
import jax.numpy as jnp
from jax import lax
from jax.experimental import pallas as pl
from jax.experimental.pallas import tpu as pltpu
from jax.sharding import PartitionSpec as P

D = 384
FF = 1536
HD = 64
NI = 6
SEQ = 197
R = 208
T = NI * R
CH = 624
NCH = T // CH
BLK = 640
JOINT, MERGE, VEC, EXPAND, REDUCE = 0, 144, 192, 256, 448
NORM_EPS = 1e-6
F32 = jnp.float32
BF16 = jnp.bfloat16
MESH = pl.DeviceIdType.MESH
HOPS = (1, 3, 2)


def dot(a, b):
    return lax.dot_general(a, b, (((1,), (0,)), ((), ())), preferred_element_type=F32)


def dot_nt(a, b):
    return lax.dot_general(a, b, (((1,), (1,)), ((), ())), preferred_element_type=F32)


def dot_tn(a, b):
    return lax.dot_general(a, b, (((0,), (0,)), ((), ())), preferred_element_type=F32)


def normalize(v):
    centered = v - jnp.mean(v, axis=-1, keepdims=True)
    variance = jnp.mean(centered * centered, axis=-1, keepdims=True)
    rstd = lax.rsqrt(variance + NORM_EPS)
    return centered * rstd, rstd


def gelu_pair(u):
    z = jnp.abs(u)
    d = 1.0 + (0.3275911 * 0.7071067811865476) * z
    t = 1.0 / d
    e = jnp.exp(-0.5 * (u * u))
    poly = ((((0.5 * 1.061405429) * t - 0.5 * 1.453152027) * t + 0.5 * 1.421413741) * t
            - 0.5 * 0.284496736) * t + 0.5 * 0.254829592
    half = poly * t * e
    phi = jnp.where(u < 0, half, 1.0 - half)
    return u * phi, phi + u * (e * 0.3989422804014327)


def norm_back(dy, xhat, rstd, gain):
    dxh = dy * gain
    m1 = jnp.mean(dxh, axis=-1, keepdims=True)
    m2 = jnp.mean(dxh * xhat, axis=-1, keepdims=True)
    return rstd * (dxh - m1 - xhat * m2)


class Place:
    def __init__(self):
        r = lax.axis_index("replica")
        s = lax.axis_index("shard")
        self.c = lax.rem(r, 2)
        self.xlo = lax.rem(lax.div(r, 2), 2)
        self.z = lax.div(r, 4)
        self.xhi = lax.rem(s, 2)
        self.y = lax.div(s, 2)
        self.x = self.xhi * 2 + self.xlo
        self.twin = self.xhi * 2 + 1 - self.xlo

    def at(self, **change):
        q = dict(x=self.x, y=self.y, z=self.z, c=self.c, **{})
        q.update(change)
        return (q["z"] * 4 + lax.rem(q["x"], 2) * 2 + q["c"], q["y"] * 2 + lax.div(q["x"], 2))

    def step(self, axis, d):
        return lax.rem(getattr(self, axis) + d, 4)

    def partner(self):
        return self.at(c=1 - self.c)

    def across(self):
        return self.at(x=3 - self.x)


def lanes(t):
    return pl.ds(128 * t, 128)


def span(start, n):
    return pl.ds(pl.multiple_of(start, 16), n)


class Group:
    def __init__(self, p, l, g0, n):
        self.p, self.l, self.g0, self.n, self.h = p, l, g0, n, n // 2

    def a_rows(self, xlo, c=None):
        return span(self.base(c) + xlo * (self.n // 4), self.n // 4)

    def b_rows(self, z, c=None):
        return span(self.base(c) + z * (self.n // 8), self.n // 8)

    def c_rows(self, c=None):
        return span(self.base(c), self.h)

    def base(self, c=None):
        return self.g0 + (self.p.c if c is None else c) * self.h


class Messages:
    def __init__(self, send, recv):
        self.send, self.recv, self.n, self.made = send, recv, 0, []

    def new(self, src, dst, dev):
        k = self.n
        self.n += 1

        def build():
            return pltpu.make_async_remote_copy(
                src_ref=src(), dst_ref=dst(), send_sem=self.send.at[k], recv_sem=self.recv.at[k],
                device_id=dev(), device_id_type=MESH)

        self.made.append(build)
        return build


def start(*groups):
    for group in groups:
        for build in group:
            build().start()


def arrive(*groups):
    for group in groups:
        for build in group:
            build().wait_recv()


class Fetch:
    def __init__(self, p, g, msgs, w):
        self.g = g
        wl = w.at[g.l]
        s = slice(None)
        ra, rb, rc = (lambda v=None: g.a_rows(p.xlo if v is None else v),
                      lambda v=None: g.b_rows(p.z if v is None else v), lambda: g.c_rows())
        ha = lambda: wl.at[p.y, p.xhi, ra(), lanes(0)]
        hb = lambda: wl.at[p.y, p.xhi, rb(), lanes(1)]
        hc = lambda: wl.at[p.y, p.xhi, rc(), lanes(2)]
        ydev = lambda d: (lambda: p.at(y=p.step("y", d)))
        xdev = lambda d: (lambda: p.at(x=p.step("x", d)))
        zdev = lambda d: (lambda: p.at(z=p.step("z", d)))
        self.c1 = [msgs.new(hc, hc, p.across)]
        self.a1 = [msgs.new(ha, ha, ydev(d)) for d in HOPS]
        self.b1 = [msgs.new(hb, hb, ydev(d)) for d in HOPS]
        ax = lambda x: (lambda: wl.at[s, lax.div(x(), 2), ra(lax.rem(x(), 2)), lanes(0)])
        cy = lambda y: (lambda: wl.at[y(), s, rc(), lanes(2)])
        bz = lambda z: (lambda: wl.at[s, s, rb(z()), lanes(1)])
        bx = lambda: wl.at[s, p.xhi, rb(), lanes(1)]
        x0, y0, z0 = (lambda: p.x), (lambda: p.y), (lambda: p.z)
        self.a2 = [msgs.new(ax(x0), ax(x0), xdev(d)) for d in HOPS]
        self.c2 = [msgs.new(cy(y0), cy(y0), ydev(d)) for d in HOPS]
        self.b2 = [msgs.new(bx, bx, p.across)]
        self.b3 = [msgs.new(bz(z0), bz(z0), zdev(d)) for d in HOPS]
        fw = lambda r: msgs.new(r, r, p.partner)
        back = lambda axis, d: (lambda: p.step(axis, (4 - d) % 4))
        self.fa = [fw(ax(back("x", d))) for d in (0,) + HOPS]
        self.fb = [fw(bz(back("z", d))) for d in (0,) + HOPS]
        self.fc = [fw(cy(back("y", d))) for d in (0,) + HOPS]

    def s1(self):
        start(self.c1, self.a1, self.b1)

    def s2(self):
        arrive(self.c1)
        start(self.c2)
        arrive(self.b1)
        start(self.b2)
        arrive(self.a1)
        start(self.a2, self.fa[:1])

    def s3(self):
        arrive(self.b2)
        start(self.b3, self.fb[:1], self.fc[:1])

    def s4(self):
        for k in range(3):
            for got, pass_on in ((self.c2, self.fc), (self.a2, self.fa), (self.b3, self.fb)):
                arrive(got[k:k + 1])
                start(pass_on[k + 1:k + 2])

    def done(self):
        arrive(self.fa, self.fb, self.fc)


class Reduce:
    def __init__(self, p, g, msgs, grad, total, cr, a, b, c):
        self.p, self.g = p, g
        s = slice(None)
        n4, n8, h = g.n // 4, g.n // 8, g.h
        gl = grad.at[g.l]
        tl = total.at[g.l]
        self.gl_ref, self.tl, self.cr = gl, tl, cr
        self.a, self.b, self.c = a, b, c
        hi, lo = (lambda v: lax.div(v, 2)), (lambda v: lax.rem(v, 2))
        go = lambda axis, d: (lambda: p.step(axis, d))
        dev = lambda axis, d: (lambda: p.at(**{axis: p.step(axis, d)}))
        other = lambda: 1 - p.c
        self.swap = {}
        for d in HOPS + (0,):
            x, y, z = go("x", d), go("y", d), go("z", d)
            self.swap[0, d] = msgs.new(
                lambda x=x: gl.at[s, hi(x()), g.a_rows(lo(x()), other()), lanes(0)],
                lambda x=x: cr.at[s, hi(x()), span(lo(x()) * n4, n4), lanes(0)], p.partner)
            self.swap[1, d] = msgs.new(
                lambda z=z: gl.at[s, s, g.b_rows(z(), other()), lanes(1)],
                lambda z=z: cr.at[s, s, span(z() * n8, n8), lanes(1)], p.partner)
            self.swap[2, d] = msgs.new(
                lambda y=y: gl.at[y(), s, g.c_rows(other()), lanes(2)],
                lambda y=y: cr.at[y(), s, pl.ds(0, h), lanes(2)], p.partner)
        self.first = {}
        for d in HOPS:
            x, y, z = go("x", d), go("y", d), go("z", d)
            self.first[0, d] = msgs.new(
                lambda x=x: gl.at[s, hi(x()), g.a_rows(lo(x())), lanes(0)],
                lambda d=d: a[0].at[d - 1], dev("x", d))
            self.first[1, d] = msgs.new(
                lambda z=z: gl.at[s, s, g.b_rows(z()), lanes(1)],
                lambda d=d: b[0].at[d - 1], dev("z", d))
            self.first[2, d] = msgs.new(
                lambda y=y: gl.at[y(), s, g.c_rows(), lanes(2)],
                lambda d=d: c[0].at[d - 1], dev("y", d))
        self.second = []
        self.third = []
        self.share = []
        for d in HOPS:
            x, y = go("x", d), go("y", d)
            self.second.append(msgs.new(
                lambda y=y: gl.at[y(), p.xhi, g.a_rows(p.xlo), lanes(0)],
                lambda d=d: a[1].at[d - 1], dev("y", d)))
            self.second.append(msgs.new(
                lambda y=y: gl.at[y(), s, g.b_rows(p.z), lanes(1)],
                lambda d=d: b[1].at[d - 1], dev("y", d)))
            self.second.append(msgs.new(
                lambda x=x: gl.at[p.y, hi(x()), g.c_rows(), lanes(2)],
                lambda: c[1].at[p.x], dev("x", d)))
            self.third.append(msgs.new(lambda: a[2].at[p.z], lambda: a[2].at[p.z], dev("z", d)))
            self.third.append(msgs.new(lambda x=x: b[2].at[hi(x())], lambda: b[3].at[p.x], dev("x", d)))
            self.third.append(msgs.new(lambda: c[2].at[p.z], lambda: c[2].at[p.z], dev("z", d)))
            rb = lambda: tl.at[g.b_rows(p.z), lanes(1)]
            self.share.append(msgs.new(rb, rb, dev("z", d)))
        ra = lambda: tl.at[g.a_rows(p.xlo), lanes(0)]
        self.share.append(msgs.new(ra, ra, lambda: p.at(x=p.twin)))
        rc = lambda: tl.at[g.c_rows(), :]
        self.final = [msgs.new(rc, rc, p.partner)]

    def begin(self):
        for d in HOPS + (0,):
            start([self.swap[t, d] for t in range(3)])

    def s1(self):
        p, g, grad, cr, l = self.p, self.g, self.gl_ref, self.cr, self.g.l
        n4, n8, h = g.n // 4, g.n // 8, g.h

        def add(gi, ci):
            grad[gi] = (grad[gi].astype(F32) + cr[ci].astype(F32)).astype(BF16)

        for d in HOPS + (0,):
            x, y, z = p.step("x", d), p.step("y", d), p.step("z", d)
            arrive([self.swap[0, d]])

            @pl.loop(0, 4)
            def _(k):
                add((k, lax.div(x, 2), g.a_rows(lax.rem(x, 2)), lanes(0)),
                    (k, lax.div(x, 2), span(lax.rem(x, 2) * n4, n4), lanes(0)))

            if d:
                start([self.first[0, d]])
            arrive([self.swap[1, d]])

            @pl.loop(0, 4)
            def _(k):
                for j in range(2):
                    add((k, j, g.b_rows(z), lanes(1)), (k, j, span(z * n8, n8), lanes(1)))

            if d:
                start([self.first[1, d]])
            arrive([self.swap[2, d]])

            @pl.loop(0, 2)
            def _(k):
                add((y, k, g.c_rows(), lanes(2)), (y, k, pl.ds(0, h), lanes(2)))

            if d:
                start([self.first[2, d]])

    def s2(self):
        p, g, grad, l = self.p, self.g, self.gl_ref, self.g.l
        arrive([self.first[0, d] for d in HOPS])

        def add(gi, ref, tail):
            v = grad[gi].astype(F32)
            for k in range(3):
                v = v + ref[(k,) + tail].astype(F32)
            grad[gi] = v.astype(BF16)

        @pl.loop(0, 4)
        def _(k):
            add((k, p.xhi, g.a_rows(p.xlo), lanes(0)), self.a[0], (k,))

        start(self.second[0::3])
        arrive([self.first[1, d] for d in HOPS])

        @pl.loop(0, 4)
        def _(k):
            for j in range(2):
                add((k, j, g.b_rows(p.z), lanes(1)), self.b[0], (k, j))

        start(self.second[1::3])
        arrive([self.first[2, d] for d in HOPS])

        @pl.loop(0, 2)
        def _(k):
            add((p.y, k, g.c_rows(), lanes(2)), self.c[0], (k,))

        start(self.second[2::3])
        self.c[1][p.x] = grad[p.y, p.xhi, g.c_rows(), lanes(2)]

    def s3(self):
        p, g, grad = self.p, self.g, self.gl_ref
        arrive(self.second[0::3])
        v = grad[p.y, p.xhi, g.a_rows(p.xlo), lanes(0)].astype(F32)
        for k in range(3):
            v = v + self.a[1][k].astype(F32)
        self.a[2][p.z] = v.astype(BF16)
        start(self.third[0::3])
        arrive(self.second[1::3])
        for j in range(2):
            v = grad[p.y, j, g.b_rows(p.z), lanes(1)].astype(F32)
            for k in range(3):
                v = v + self.b[1][k, j].astype(F32)
            self.b[2][j] = v.astype(BF16)
        start(self.third[1::3])
        self.b[3][p.x] = self.b[2][p.xhi]
        arrive(self.second[2::3])
        v = self.c[1][0].astype(F32)
        for k in range(1, 4):
            v = v + self.c[1][k].astype(F32)
        self.c[2][p.z] = v.astype(BF16)
        start(self.third[2::3])

    def s4(self):
        p, g, tl = self.p, self.g, self.tl

        def total(ref):
            v = ref[0].astype(F32)
            for k in range(1, 4):
                v = v + ref[k].astype(F32)
            return v.astype(BF16)

        arrive(self.third[0::3])
        tl[g.a_rows(p.xlo), lanes(0)] = total(self.a[2])
        start(self.share[3:])
        arrive(self.third[1::3])
        tl[g.b_rows(p.z), lanes(1)] = total(self.b[3])
        start(self.share[:3])
        arrive(self.third[2::3])
        tl[g.c_rows(), lanes(2)] = total(self.c[2])

    def s5(self):
        arrive(self.share)
        start(self.final)

    def done(self):
        arrive(self.final)


FFN_ROWS = (EXPAND, 384)
ATT_ROWS = (0, 256)
N_COMM = 12


def train_kernel(count, img, cot, joint, merge, expand, reduce_w, vec_in,
                 out, dimg, total_out, g_spill, gp_spill,
                 w, sp, xs, hs, a_s, c_s, o_s, qkv, g_s, gp_s, dx_s, dzb_s, dyb_s,
                 lse_s, grad, small, total, in_stage, *rest):
    slots, (send, recv, lsem, wsem) = rest[:4 * N_COMM], rest[4 * N_COMM:]
    p = Place()
    barrier = pltpu.get_barrier_semaphore()
    friends = [p.partner()] + [p.at(**{a: p.step(a, d)}) for a in "xyz" for d in HOPS]

    msgs = Messages(send, recv)
    F = [[Fetch(p, Group(p, l, *rows), msgs, w) for rows in (ATT_ROWS, FFN_ROWS)] for l in range(2)]
    RD = {}
    for n, (l, rows) in enumerate([(1, FFN_ROWS), (1, ATT_ROWS), (0, FFN_ROWS), (0, ATT_ROWS)]):
        q = slots[N_COMM * n:N_COMM * (n + 1)]
        cr = slots[N_COMM * (n % 2)]
        RD[l, rows] = Reduce(p, Group(p, l, *rows), msgs, grad, total, cr, q[1:4], q[4:8], q[8:11])

    pieces = []
    for l in range(2):
        for cb in range(3):
            pieces.append((l, joint.at[l, :, pl.ds(D * cb, D)], JOINT + 48 * cb, 48))
        pieces.append((l, merge.at[l], MERGE, 48))
        pieces.append((l, vec_in.at[l], VEC, 16))
        for cb in range(4):
            pieces.append((l, expand.at[l, :, pl.ds(D * cb, D)], EXPAND + 48 * cb, 48))
        pieces.append((l, reduce_w.at[l], REDUCE, 192))
    loads = [pltpu.make_async_copy(src, hs.at[l, pl.ds(at, n), :], wsem.at[k])
             for k, (l, src, at, n) in enumerate(pieces)]
    for cp in loads:
        cp.start()
    get_img = pltpu.make_async_copy(img, in_stage, lsem.at[3])
    get_img.start()
    for k, cp in enumerate(loads):
        cp.wait()
        if k % 10 == 9:
            l = k // 10
            for at, n in ((0, VEC + 16), (EXPAND, BLK - EXPAND)):
                w[l, p.y, p.xhi, pl.ds(at, n), :] = hs[l, pl.ds(at, n), :].astype(BF16)
    for dev in friends:
        pl.semaphore_signal(barrier, inc=1, device_id=dev, device_id_type=MESH)
    pl.semaphore_wait(barrier, len(friends))

    f = F[0][0]
    f.s1()

    n_live = count[0]

    def rows_of(c):
        return pl.ds(pl.multiple_of(c * CH, CH), CH)

    def img_rows(i, n=R):
        return pl.ds(pl.multiple_of(i * R, R), n)

    def tail_rows(i):
        return pl.ds(pl.multiple_of(i * R, R) + 192, 16)

    get_img.wait()

    @pl.loop(0, NI)
    def _(i):
        xs[0, tail_rows(i), :] = jnp.zeros((16, D), F32)
        xs[0, img_rows(i, SEQ), :] = in_stage[i].astype(F32)

    get_cot = pltpu.make_async_copy(cot, in_stage, lsem.at[3])
    get_cot.start()
    f.s2()
    f.s3()
    f.s4()
    f.done()

    lane = lax.broadcasted_iota(jnp.int32, (R, 128), 1)
    row = lax.broadcasted_iota(jnp.int32, (R, 128), 0)
    mine = [lane < HD, lane >= HD]
    spare = [lane == HD, lane == 0]
    key_fill = [jnp.where(v & (row >= SEQ), -1e30, 0.0).astype(BF16) for v in spare]
    query_fill = [jnp.where(v, 1.0, 0.0).astype(BF16) for v in spare]
    blank = jnp.zeros((R, 128), BF16)
    ones = jnp.ones((16, R), BF16)

    def pieces_of(first, n):
        got, at = [], first
        while at < first + n:
            m = min(D - at % D, first + n - at)
            got.append((at // D, at % D, m))
            at += m
        return got

    def weight(l, at, first=0, n=D):
        parts = [w[l, :, :, pl.ds(at + 48 * k, 48), pl.ds(lane0, m)].reshape(D, m)
                 for k, lane0, m in pieces_of(first, n)]
        return parts[0] if len(parts) == 1 else jnp.concatenate(parts, axis=1)

    def put_grad_cols(l, at, first, val):
        done = 0
        for k, lane0, m in pieces_of(first, val.shape[1]):
            grad[l, :, :, pl.ds(at + 48 * k, 48), pl.ds(lane0, m)] = (
                val[:, done:done + m].astype(BF16).reshape(4, 2, 48, m))
            done += m

    def reduce_rows(l, first, n):
        got, at = [], first
        while at < first + n:
            m = min(192 - at % 192, first + n - at)
            s = at // 192
            got.append(w[l, s // 2, s % 2, pl.ds(REDUCE + at % 192, m), :])
            at += m
        return jnp.concatenate(got, axis=0)

    THIRDS = ((0, 512), (512, 512), (1024, 128))
    FW = 512


    plan = {}

    def during(phase, l, step, *calls):
        plan.setdefault((phase, l), {}).setdefault(step, []).extend(calls)

    def run(phase, l, n, body):
        at = plan.get((phase, l), {})

        def one(i, _):
            for step, calls in at.items():
                @pl.when(i == step)
                def _():
                    for call in calls:
                        call()
            body(i)
            return 0

        lax.fori_loop(0, n, one, 0)

    during("p1", 0, 0, F[0][1].s1)
    during("p2", 0, 0, F[0][1].s2)
    during("p2", 0, 1, F[0][1].s3)
    during("p2", 0, 2, F[0][1].s4, F[1][0].s1)
    during("p3", 0, 0, F[1][0].s2, F[1][0].s3, F[1][1].s1)
    during("p3", 0, 1, F[1][0].s4, F[1][1].s2)
    during("p1", 1, 1, F[1][1].s3)
    during("p2", 1, 2, F[1][1].s4)

    spills = [(g_s, g_spill, lsem.at[4]), (gp_s, gp_spill, lsem.at[5])]

    for l in range(2):
        if l:
            F[1][0].done()
        acc = w[l, 0, 0, pl.ds(VEC, 16), :].astype(F32)
        for s in range(1, 8):
            acc = acc + w[l, s // 2, s % 2, pl.ds(VEC, 16), :].astype(F32)
        sp[l] = acc
        vec = lambda r: sp[l, r:r + 1, :]

        def p1(c):
            rows = rows_of(c)
            xhat, _r = normalize(xs[l, rows, :])
            a = (xhat * vec(0) + vec(1)).astype(BF16)
            a_s[l, rows, :] = a
            for first, n in THIRDS:
                val = dot(a, weight(l, JOINT, first, n))
                if first == 0:
                    val = jnp.concatenate([val[:, :D] * (HD ** -0.5), val[:, D:]], axis=1)
                qkv[l, rows, pl.ds(first, n)] = val.astype(BF16)

        run("p1", l, NCH, p1)

        def p2(k):
            heads = [(2 * k + u, j, e) for u in range(2) for j in range(3) for e in range(2)]
            scores, tops, weights, parts = [], [], [], []
            for i, j, e in heads:
                rows = img_rows(i)
                q2 = qkv[l, rows, pl.ds(128 * j, 128)]
                k2 = qkv[l, rows, pl.ds(D + 128 * j, 128)]
                scores.append(dot_nt(jnp.where(mine[e], k2, key_fill[e]),
                                     jnp.where(mine[e], q2, query_fill[e])))
            for st in scores:
                tops.append(jnp.max(st, axis=0, keepdims=True))
                weights.append(jnp.exp(st - tops[-1]).astype(BF16))
            for n, (i, j, e) in enumerate(heads):
                rows = img_rows(i)
                if e == 0:
                    v2t = qkv[l, rows, pl.ds(2 * D + 128 * j, 128)].T
                val = dot(jnp.concatenate([v2t[HD * e:HD * (e + 1), :], ones], axis=0), weights[n])
                tot = val[HD:HD + 1, :]
                lse_s[l, i, 2 * j + e:2 * j + e + 1, :] = tops[n] + jnp.log(tot)
                parts.append(val[:HD, :] * (1.0 / tot))
                if e == 1:
                    o_s[l, rows, pl.ds(128 * j, 128)] = jnp.concatenate(parts[-2:], axis=0).T.astype(BF16)

        run("p2", l, NI // 2, p2)

        F[l][1].done()
        if l:
            for src, dst, sem in spills:
                pltpu.make_async_copy(src, dst, sem).wait()

        def p3(c):
            rows = rows_of(c)
            h = xs[l, rows, :] + dot(o_s[l, rows, :], weight(l, MERGE))
            hs[l, rows, :] = h
            xhat, _r = normalize(h)
            cc = (xhat * vec(2) + vec(3)).astype(BF16)
            c_s[l, rows, :] = cc
            acc = h + vec(4)
            bias = jnp.concatenate([vec(5 + k) for k in range(4)], axis=1)
            u, g = {}, {}
            for f in range(FF // FW + 2):
                if f < FF // FW:
                    u[f] = dot(cc, weight(l, EXPAND, FW * f, FW)) + bias[:, FW * f:FW * (f + 1)]
                if 1 <= f <= FF // FW:
                    val, slope = gelu_pair(u[f - 1])
                    g[f - 1] = val.astype(BF16)
                    g_s[rows, pl.ds(FW * (f - 1), FW)] = g[f - 1]
                    gp_s[rows, pl.ds(FW * (f - 1), FW)] = slope.astype(BF16)
                if f >= 2:
                    acc = acc + dot(g[f - 2], reduce_rows(l, FW * (f - 2), FW))
            if l == 0:
                xs[1, rows, :] = acc
            else:
                for k in range(CH // R):
                    i = c * (CH // R) + k
                    live = jnp.where(i < n_live, 1.0, 0.0).astype(F32)
                    dx_s[img_rows(i), :] = acc[R * k:R * (k + 1), :] * live

        run("p3", l, NCH, p3)
        if l == 0:
            for src, dst, sem in spills:
                pltpu.make_async_copy(src, dst, sem).start()

    put_out = pltpu.make_async_copy(dx_s, out, lsem.at[6])
    put_out.start()
    small[...] = jnp.zeros_like(small)
    get_cot.wait()
    put_out.wait()

    @pl.loop(0, NI)
    def _(i):
        live = jnp.where(i < n_live, 1.0, 0.0).astype(F32)
        dx_s[tail_rows(i), :] = jnp.zeros((16, D), F32)
        dx_s[img_rows(i, SEQ), :] = in_stage[i].astype(F32) * live

    R1, R2, R3, R4 = RD[1, FFN_ROWS], RD[1, ATT_ROWS], RD[0, FFN_ROWS], RD[0, ATT_ROWS]
    during("b2", 1, 2, R1.s1)
    during("b3", 1, 0, R1.s2)
    during("b1", 0, 0, R1.s3, R2.s1)
    during("b1", 0, 1, R1.s4)
    during("b2", 0, 0, R2.s2, R1.s5)
    during("b2", 0, 2, R2.s3)
    during("b2", 0, 3, R3.s1)
    during("b2", 0, 5, R2.s4)
    during("b3", 0, 1, R3.s2, R2.s5)

    def colsum(v):
        return jnp.sum(v, axis=0, keepdims=True)

    for l in (1, 0):
        vec = lambda r: sp[l, r:r + 1, :]
        if l == 0:
            for dst, src, sem in spills:
                pltpu.make_async_copy(src, dst, sem).wait()

        def b1(c):
            rows = rows_of(c)
            dx = dx_s[rows, :]
            dzb = dx.astype(BF16)
            dzb_s[rows, :] = dzb
            small[l, 4:5, :] += colsum(dzb.astype(F32))
            dg = {}
            for f in range(FF // FW + 1):
                if f < FF // FW:
                    dg[f] = dot_nt(dzb, reduce_rows(l, FW * f, FW))
                if f >= 1:
                    at = pl.ds(FW * (f - 1), FW)
                    gp_s[rows, at] = (dg[f - 1] * gp_s[rows, at].astype(F32)).astype(BF16)
            for k in range(4):
                small[l, 5 + k:6 + k, :] += colsum(gp_s[rows, pl.ds(D * k, D)].astype(F32))
            dc = dot_nt(gp_s[rows, :], weight(l, EXPAND, 0, FF))
            xhat, rstd = normalize(hs[l, rows, :])
            small[l, 2:3, :] += colsum(dc * xhat)
            small[l, 3:4, :] += colsum(dc)
            dh = dx + norm_back(dc, xhat, rstd, vec(2))
            dx_s[rows, :] = dh
            dyb = dh.astype(BF16)
            dyb_s[rows, :] = dyb
            hs[l, rows, :] = dot_nt(dyb, weight(l, MERGE))

        run("b1", l, NCH, b1)

        for f in range(FF // FW):
            put_grad_cols(l, EXPAND, FW * f, dot_tn(c_s[l], gp_s[:, pl.ds(FW * f, FW)]))
        for f in (0, 2):
            val = dot_tn(dzb_s[...], g_s[:, pl.ds(D * f, 2 * D)])
            grad[l, f, :, pl.ds(REDUCE, 192), :] = val[:, :D].T.astype(BF16).reshape(2, 192, D)
            grad[l, f + 1, :, pl.ds(REDUCE, 192), :] = val[:, D:].T.astype(BF16).reshape(2, 192, D)
        RD[l, FFN_ROWS].begin()
        if l:
            for dst, src, sem in spills:
                pltpu.make_async_copy(src, dst, sem).start()
        put_grad_cols(l, MERGE, 0, dot_tn(o_s[l], dyb_s[...]))

        def b2(i):
            rows = img_rows(i)
            heads = [(j, e) for j in range(3) for e in range(2)]
            scores, slopes, weights, down_scores = [], [], [], []
            dq, dk, dv, down = [], [], [], []
            for j, e in heads:
                q2 = qkv[l, rows, pl.ds(128 * j, 128)]
                k2 = qkv[l, rows, pl.ds(D + 128 * j, 128)]
                v2 = qkv[l, rows, pl.ds(2 * D + 128 * j, 128)]
                do2 = hs[l, rows, pl.ds(128 * j, 128)].astype(BF16)
                down.append(do2)
                scores.append(dot_nt(jnp.where(mine[e], k2, key_fill[e]),
                                     jnp.where(mine[e], q2, query_fill[e])))
                slopes.append(dot_nt(v2, jnp.where(mine[e], do2, blank)))
            for n, (j, e) in enumerate(heads):
                pt = jnp.exp(scores[n] - lse_s[l, i, n:n + 1, :])
                r = jnp.sum(slopes[n] * pt, axis=0, keepdims=True)
                weights.append(pt.astype(BF16))
                down_scores.append((pt * (slopes[n] - r)).astype(BF16))
            for n, (j, e) in enumerate(heads):
                if e == 0:
                    k2t = qkv[l, rows, pl.ds(D + 128 * j, 128)].T
                dv.append(dot(weights[n], down[n]))
                dk.append(dot(down_scores[n], qkv[l, rows, pl.ds(128 * j, 128)]))
                dq.append(dot(k2t[HD * e:HD * (e + 1), :], down_scores[n]))
                if e == 1:
                    new_q = jnp.concatenate(dq[-2:], axis=0).T * (HD ** -0.5)
                    qkv[l, rows, pl.ds(128 * j, 128)] = new_q.astype(BF16)
                    qkv[l, rows, pl.ds(D + 128 * j, 128)] = jnp.where(mine[0], *dk[-2:]).astype(BF16)
                    qkv[l, rows, pl.ds(2 * D + 128 * j, 128)] = jnp.where(mine[0], *dv[-2:]).astype(BF16)

        run("b2", l, NI, b2)

        def b3(c):
            rows = rows_of(c)
            da = dot_nt(qkv[l, rows, :], weight(l, JOINT, 0, 3 * D))
            xhat, rstd = normalize(xs[l, rows, :])
            small[l, 0:1, :] += colsum(da * xhat)
            small[l, 1:2, :] += colsum(da)
            dx = dx_s[rows, :] + norm_back(da, xhat, rstd, vec(0))
            dx_s[rows, :] = dx

        run("b3", l, NCH, b3)

        for s in range(8):
            grad[l, s // 2, s % 2, pl.ds(VEC, 16), :] = small[l].astype(BF16)
        for first, n in THIRDS:
            put_grad_cols(l, JOINT, first, dot_tn(a_s[l], qkv[l, :, pl.ds(first, n)]))
        RD[l, ATT_ROWS].begin()

    put_grad = pltpu.make_async_copy(dx_s, dimg, lsem.at[6])
    put_grad.start()
    R3.s3()
    R4.s1()
    R3.s4()
    R4.s2()
    R3.s5()
    R4.s3()
    R4.s4()
    R4.s5()
    for rd in (R1, R2, R3, R4):
        rd.done()
    put_total = pltpu.make_async_copy(total, total_out, lsem.at[7])
    put_total.start()
    for build in msgs.made:
        build().wait_send()
    put_grad.wait()
    put_total.wait()


def train(count, img, cot, joint, merge, expand, reduce_w, vec):
    A = pl.BlockSpec(memory_space=pl.ANY)
    vm = lambda *shape: pltpu.VMEM(shape, BF16)
    vf = lambda *shape: pltpu.VMEM(shape, F32)
    slots = []
    for k, n in enumerate((384, 256, 384, 256)):
        n4, n8, h = n // 4, n // 8, n // 2
        slots += [vm(4, 2, h, D) if k < 2 else vm(16, 128),
                  vm(3, 4, n4, 128), vm(3, n4, 128), vm(4, n4, 128),
                  vm(3, 4, 2, n8, 128), vm(3, 2, n8, 128), vm(2, n8, 128), vm(4, n8, 128),
                  vm(3, 2, h, 128), vm(4, h, 128), vm(4, h, 128), vm(16, 128)]
    return pl.pallas_call(
        train_kernel,
        out_shape=(
            jax.ShapeDtypeStruct((T, D), F32),
            jax.ShapeDtypeStruct((T, D), F32),
            jax.ShapeDtypeStruct((2, BLK, D), BF16),
            jax.ShapeDtypeStruct((T, FF), BF16),
            jax.ShapeDtypeStruct((T, FF), BF16),
        ),
        in_specs=[pl.BlockSpec(memory_space=pltpu.SMEM)] + [A] * 7,
        out_specs=(A,) * 5,
        scratch_shapes=[
            vm(2, 4, 2, BLK, D), vf(2, 16, D),
            vf(2, T, D), vf(2, T, D),
            vm(2, T, D), vm(2, T, D), vm(2, T, D),
            vm(2, T, 3 * D), vm(T, FF), vm(T, FF),
            vf(T, D), vm(T, D), vm(T, D),
            vf(2, NI, 8, R),
            vm(2, 4, 2, BLK, D), vf(2, 16, D), vm(2, BLK, D),
            vm(NI, SEQ, D),
            *slots,
            pltpu.SemaphoreType.DMA((N_SEMS,)), pltpu.SemaphoreType.DMA((N_SEMS,)),
            pltpu.SemaphoreType.DMA((8,)), pltpu.SemaphoreType.DMA((20,)),
        ],
        compiler_params=pltpu.CompilerParams(collective_id=0, has_side_effects=True,
                                             vmem_limit_bytes=65200 * 1024),
        cost_estimate=pl.CostEstimate(flops=28_000_000_000, bytes_accessed=20_000_000,
                                      transcendentals=8_000_000),
    )(count, img, cot, joint, merge, expand, reduce_w, vec)


N_SEMS = 4 * 29 + 4 * 44


BETA_ONE = 0.9
BETA_TWO = 0.999
ADAM_EPS = 1e-08
DECAY_MATRIX = 0.05
RATE_MATRIX = 0.05
RATE_SMALL = 0.4
STEP = 10


def adam_update(gradient, first_moment, second_moment, master, step_rate, decay_rate):
    first_new = BETA_ONE * first_moment + (1.0 - BETA_ONE) * gradient
    second_new = BETA_TWO * second_moment + (1.0 - BETA_TWO) * gradient * gradient
    corrected = first_new / (1.0 - BETA_ONE**STEP)
    denominator = jnp.sqrt(second_new / (1.0 - BETA_TWO**STEP)) + ADAM_EPS
    master_new = master - step_rate * (corrected / denominator + decay_rate * master)
    return (first_new, second_new, master_new)


def adam_kernel(g, *refs):
    ins, outs = refs[:12], refs[12:]
    for kind, (at, blocks, rows) in enumerate(
            [(JOINT, 3, 48), (MERGE, 1, 48), (EXPAND, 4, 48), (REDUCE, 1, 192)]):
        for cb in range(blocks):
            grad = g[0, pl.ds(at + 48 * cb, rows), :].astype(F32)
            cols = (0, slice(None), pl.ds(D * cb, D))
            m, v, wt = (ins[3 * kind + k][cols] for k in range(3))
            new = adam_update(grad, m, v, wt, RATE_MATRIX, DECAY_MATRIX)
            for k, val in enumerate((grad,) + new):
                outs[4 * kind + k][cols] = val


def adam(g, firsts, seconds, masters):
    widths = (3 * D, D, 4 * D, D)
    rows = (48, 48, 48, 192)
    spec = [pl.BlockSpec((1, r, wd), lambda l: (l, 0, 0)) for r, wd in zip(rows, widths)]
    ins, in_specs, out_specs, shapes = [], [], [], []
    for k in range(4):
        for a in (firsts[k], seconds[k], masters[k]):
            ins.append(a)
            in_specs.append(spec[k])
        for _ in range(4):
            out_specs.append(spec[k])
            shapes.append(jax.ShapeDtypeStruct(masters[k].shape, F32))
    return pl.pallas_call(
        adam_kernel,
        grid=(2,),
        out_shape=tuple(shapes),
        in_specs=[pl.BlockSpec((1, BLK, D), lambda l: (l, 0, 0))] + in_specs,
        out_specs=tuple(out_specs),
        compiler_params=pltpu.CompilerParams(vmem_limit_bytes=32 * 1024 * 1024),
    )(g, *ins)


def shards(images, cotangent, image_count, joint_weight, merge_weight, expand_weight,
           reduce_weight, small_params, joint_first, merge_first, expand_first, reduce_first,
           small_first, joint_second, merge_second, expand_second, reduce_second, small_second):
    masters = (joint_weight, merge_weight, expand_weight, reduce_weight)
    firsts = (joint_first, merge_first, expand_first, reduce_first)
    seconds = (joint_second, merge_second, expand_second, reduce_second)
    width = small_params.shape[1]
    rank = lax.axis_index("shard")
    vec = lax.dynamic_update_slice_in_dim(jnp.zeros((2, 16 * D), F32), small_params, rank * width, 1)
    block_out, image_grad, total, _g, _gp = train(
        image_count, images, cotangent, *masters, vec.reshape(2, 16, D))
    done = adam(total, firsts, seconds, masters)
    vec_grad = lax.dynamic_slice_in_dim(total[:, VEC:VEC + 9].reshape(2, 9 * D), rank * width, width, 1)
    vec_grad = vec_grad.astype(F32)
    vec_done = (vec_grad,) + adam_update(vec_grad, small_first, small_second, small_params,
                                         RATE_SMALL, 0.0)
    outputs = [v.reshape(NI, R, D)[:, :SEQ] for v in (block_out, image_grad)]
    for member in range(4):
        outputs += [done[4 * kind + member] for kind in range(4)] + [vec_done[member]]
    return tuple(outputs)


def solution(mesh):
    whole = P(("replica", "shard"), None, None)
    weights = [P(None, "shard", None)] * 4 + [P(None, "shard")]
    return jax.shard_map(
        shards,
        mesh=mesh,
        in_specs=(whole, whole, P(("replica", "shard"))) + tuple(weights * 3),
        out_specs=(whole, whole) + tuple(weights * 4),
        check_vma=False,
    )
```

```python
import jax
import jax.numpy as jnp
from jax import lax
from jax.experimental import pallas as pl
from jax.experimental.pallas import tpu as pltpu
from jax.sharding import PartitionSpec as P

D = 384
FF = 1536
HD = 64
NI = 6
SEQ = 197
R = 208
T = NI * R
CH = 624
NCH = T // CH
BLK = 640
JOINT, MERGE, VEC, EXPAND, REDUCE = 0, 144, 192, 256, 448
NORM_EPS = 1e-6
F32 = jnp.float32
BF16 = jnp.bfloat16
MESH = pl.DeviceIdType.MESH
HOPS = (1, 3, 2)


def dot(a, b):
    return lax.dot_general(a, b, (((1,), (0,)), ((), ())), preferred_element_type=F32)


def dot_nt(a, b):
    return lax.dot_general(a, b, (((1,), (1,)), ((), ())), preferred_element_type=F32)


def dot_tn(a, b):
    return lax.dot_general(a, b, (((0,), (0,)), ((), ())), preferred_element_type=F32)


def normalize(v):
    centered = v - jnp.mean(v, axis=-1, keepdims=True)
    variance = jnp.mean(centered * centered, axis=-1, keepdims=True)
    rstd = lax.rsqrt(variance + NORM_EPS)
    return centered * rstd, rstd


def gelu_pair(u):
    z = jnp.abs(u)
    d = 1.0 + (0.3275911 * 0.7071067811865476) * z
    t = 1.0 / d
    e = jnp.exp(-0.5 * (u * u))
    poly = ((((0.5 * 1.061405429) * t - 0.5 * 1.453152027) * t + 0.5 * 1.421413741) * t
            - 0.5 * 0.284496736) * t + 0.5 * 0.254829592
    half = poly * t * e
    phi = jnp.where(u < 0, half, 1.0 - half)
    return u * phi, phi + u * (e * 0.3989422804014327)


def norm_back(dy, xhat, rstd, gain):
    dxh = dy * gain
    m1 = jnp.mean(dxh, axis=-1, keepdims=True)
    m2 = jnp.mean(dxh * xhat, axis=-1, keepdims=True)
    return rstd * (dxh - m1 - xhat * m2)


class Place:
    def __init__(self):
        r = lax.axis_index("replica")
        s = lax.axis_index("shard")
        self.c = lax.rem(r, 2)
        self.xlo = lax.rem(lax.div(r, 2), 2)
        self.z = lax.div(r, 4)
        self.xhi = lax.rem(s, 2)
        self.y = lax.div(s, 2)
        self.x = self.xhi * 2 + self.xlo
        self.twin = self.xhi * 2 + 1 - self.xlo

    def at(self, **change):
        q = dict(x=self.x, y=self.y, z=self.z, c=self.c, **{})
        q.update(change)
        return (q["z"] * 4 + lax.rem(q["x"], 2) * 2 + q["c"], q["y"] * 2 + lax.div(q["x"], 2))

    def step(self, axis, d):
        return lax.rem(getattr(self, axis) + d, 4)

    def partner(self):
        return self.at(c=1 - self.c)

    def across(self):
        return self.at(x=3 - self.x)

    def friends(self):
        other = 1 - self.c
        return ([self.partner(), self.at(x=self.twin, c=other)]
                + [self.at(**{a: self.step(a, d)}) for a in "xyz" for d in HOPS]
                + [self.at(z=self.step("z", d), c=other) for d in HOPS])


def lanes(t):
    return pl.ds(128 * t, 128)


def span(start, n):
    return pl.ds(pl.multiple_of(start, 16), n)


class Group:
    def __init__(self, p, l, g0, n):
        self.p, self.l, self.g0, self.n, self.h = p, l, g0, n, n // 2

    def a_rows(self, xlo, c=None):
        return span(self.base(c) + xlo * (self.n // 4), self.n // 4)

    def b_rows(self, z, c=None):
        return span(self.base(c) + z * (self.n // 8), self.n // 8)

    def c_rows(self, c=None):
        return span(self.base(c), self.h)

    def base(self, c=None):
        return self.g0 + (self.p.c if c is None else c) * self.h


class Messages:
    def __init__(self, send, recv):
        self.send, self.recv, self.n, self.made = send, recv, 0, []

    def new(self, src, dst, dev):
        k = self.n
        self.n += 1

        def build():
            return pltpu.make_async_remote_copy(
                src_ref=src(), dst_ref=dst(), send_sem=self.send.at[k], recv_sem=self.recv.at[k],
                device_id=dev(), device_id_type=MESH)

        self.made.append(build)
        return build


def start(*groups):
    for group in groups:
        for build in group:
            build().start()


def arrive(*groups):
    for group in groups:
        for build in group:
            build().wait_recv()


class Fetch:
    def __init__(self, p, g, msgs, w):
        self.g = g
        wl = w.at[g.l]
        s = slice(None)
        ra, rb, rc = (lambda v=None: g.a_rows(p.xlo if v is None else v),
                      lambda v=None: g.b_rows(p.z if v is None else v), lambda: g.c_rows())
        ha = lambda: wl.at[p.y, p.xhi, ra(), lanes(0)]
        hb = lambda: wl.at[p.y, p.xhi, rb(), lanes(1)]
        hc = lambda: wl.at[p.y, p.xhi, rc(), lanes(2)]
        ydev = lambda d: (lambda: p.at(y=p.step("y", d)))
        xdev = lambda d: (lambda: p.at(x=p.step("x", d)))
        zdev = lambda d: (lambda: p.at(z=p.step("z", d)))
        self.c1 = [msgs.new(hc, hc, p.across)]
        self.a1 = [msgs.new(ha, ha, ydev(d)) for d in HOPS]
        self.b1 = [msgs.new(hb, hb, ydev(d)) for d in HOPS]
        ax = lambda x: (lambda: wl.at[s, lax.div(x(), 2), ra(lax.rem(x(), 2)), lanes(0)])
        cy = lambda y: (lambda: wl.at[y(), s, rc(), lanes(2)])
        bz = lambda z: (lambda: wl.at[s, s, rb(z()), lanes(1)])
        bx = lambda: wl.at[s, p.xhi, rb(), lanes(1)]
        x0, y0, z0 = (lambda: p.x), (lambda: p.y), (lambda: p.z)
        self.a2 = [msgs.new(ax(x0), ax(x0), xdev(d)) for d in HOPS]
        self.c2 = [msgs.new(cy(y0), cy(y0), ydev(d)) for d in HOPS]
        self.b2 = [msgs.new(bx, bx, p.across)]
        self.b3 = [msgs.new(bz(z0), bz(z0), zdev(d)) for d in HOPS]
        fw = lambda r: msgs.new(r, r, p.partner)
        back = lambda axis, d: (lambda: p.step(axis, (4 - d) % 4))
        self.fa = [fw(ax(back("x", d))) for d in (0,) + HOPS]
        self.fb = [fw(bz(back("z", d))) for d in (0,) + HOPS]
        self.fc = [fw(cy(back("y", d))) for d in (0,) + HOPS]

    def s1(self):
        start(self.c1, self.a1, self.b1)

    def s2(self):
        arrive(self.c1)
        start(self.c2)
        arrive(self.b1)
        start(self.b2)
        arrive(self.a1)
        start(self.a2, self.fa[:1])

    def s3(self):
        arrive(self.b2)
        start(self.b3, self.fb[:1], self.fc[:1])

    def s4(self):
        for k in range(3):
            for got, pass_on in ((self.c2, self.fc), (self.a2, self.fa), (self.b3, self.fb)):
                arrive(got[k:k + 1])
                start(pass_on[k + 1:k + 2])

    def done(self):
        arrive(self.fa, self.fb, self.fc)


class Reduce:
    def __init__(self, p, g, msgs, grad, total, cr, a, b, c):
        self.p, self.g = p, g
        s = slice(None)
        n4, n8, h = g.n // 4, g.n // 8, g.h
        gl = grad.at[g.l]
        tl = total.at[g.l]
        self.gl_ref, self.tl, self.cr = gl, tl, cr
        self.a, self.b, self.c = a, b, c
        hi, lo = (lambda v: lax.div(v, 2)), (lambda v: lax.rem(v, 2))
        go = lambda axis, d: (lambda: p.step(axis, d))
        dev = lambda axis, d: (lambda: p.at(**{axis: p.step(axis, d)}))
        other = lambda: 1 - p.c
        self.swap = {}
        for d in HOPS + (0,):
            x, y, z = go("x", d), go("y", d), go("z", d)
            self.swap[0, d] = msgs.new(
                lambda x=x: gl.at[s, hi(x()), g.a_rows(lo(x()), other()), lanes(0)],
                lambda x=x: cr.at[s, hi(x()), span(lo(x()) * n4, n4), lanes(0)], p.partner)
            self.swap[1, d] = msgs.new(
                lambda z=z: gl.at[s, s, g.b_rows(z(), other()), lanes(1)],
                lambda z=z: cr.at[s, s, span(z() * n8, n8), lanes(1)], p.partner)
            self.swap[2, d] = msgs.new(
                lambda y=y: gl.at[y(), s, g.c_rows(other()), lanes(2)],
                lambda y=y: cr.at[y(), s, pl.ds(0, h), lanes(2)], p.partner)
        self.first = {}
        for d in HOPS:
            x, y, z = go("x", d), go("y", d), go("z", d)
            self.first[0, d] = msgs.new(
                lambda x=x: gl.at[s, hi(x()), g.a_rows(lo(x())), lanes(0)],
                lambda d=d: a[0].at[d - 1], dev("x", d))
            self.first[1, d] = msgs.new(
                lambda z=z: gl.at[s, s, g.b_rows(z()), lanes(1)],
                lambda d=d: b[0].at[d - 1], dev("z", d))
            self.first[2, d] = msgs.new(
                lambda y=y: gl.at[y(), s, g.c_rows(), lanes(2)],
                lambda d=d: c[0].at[d - 1], dev("y", d))
        self.second = []
        self.third = []
        for d in HOPS:
            x, y = go("x", d), go("y", d)
            self.second.append(msgs.new(
                lambda y=y: gl.at[y(), p.xhi, g.a_rows(p.xlo), lanes(0)],
                lambda d=d: a[1].at[d - 1], dev("y", d)))
            self.second.append(msgs.new(
                lambda y=y: gl.at[y(), s, g.b_rows(p.z), lanes(1)],
                lambda d=d: b[1].at[d - 1], dev("y", d)))
            self.second.append(msgs.new(
                lambda x=x: gl.at[p.y, hi(x()), g.c_rows(), lanes(2)],
                lambda: c[1].at[p.x], dev("x", d)))
            self.third.append(msgs.new(lambda: a[2].at[p.z], lambda: a[2].at[p.z], dev("z", d)))
            self.third.append(msgs.new(lambda x=x: b[2].at[hi(x())], lambda: b[3].at[p.x], dev("x", d)))
            self.third.append(msgs.new(lambda: c[2].at[p.z], lambda: c[2].at[p.z], dev("z", d)))
        ra = lambda: tl.at[g.a_rows(p.xlo), lanes(0)]
        rb = lambda: tl.at[g.b_rows(p.z), lanes(1)]
        rc = lambda: tl.at[g.c_rows(), lanes(2)]
        self.share_a = [msgs.new(ra, ra, lambda: p.at(x=p.twin)),
                        msgs.new(ra, ra, lambda: p.at(x=p.twin, c=1 - p.c)),
                        msgs.new(ra, ra, p.partner)]
        self.share_b = [msgs.new(rb, rb, p.partner)]
        for d in HOPS:
            self.share_b.append(msgs.new(rb, rb, dev("z", d)))
            self.share_b.append(msgs.new(rb, rb, lambda d=d: p.at(z=p.step("z", d), c=1 - p.c)))
        self.share_c = [msgs.new(rc, rc, p.partner)]

    def begin(self):
        for d in HOPS + (0,):
            start([self.swap[t, d] for t in range(3)])

    def s1(self):
        p, g, grad, cr, l = self.p, self.g, self.gl_ref, self.cr, self.g.l
        n4, n8, h = g.n // 4, g.n // 8, g.h

        def add(gi, ci):
            grad[gi] = (grad[gi].astype(F32) + cr[ci].astype(F32)).astype(BF16)

        for d in HOPS + (0,):
            x, y, z = p.step("x", d), p.step("y", d), p.step("z", d)
            arrive([self.swap[0, d]])

            @pl.loop(0, 4)
            def _(k):
                add((k, lax.div(x, 2), g.a_rows(lax.rem(x, 2)), lanes(0)),
                    (k, lax.div(x, 2), span(lax.rem(x, 2) * n4, n4), lanes(0)))

            if d:
                start([self.first[0, d]])
            arrive([self.swap[1, d]])

            @pl.loop(0, 4)
            def _(k):
                for j in range(2):
                    add((k, j, g.b_rows(z), lanes(1)), (k, j, span(z * n8, n8), lanes(1)))

            if d:
                start([self.first[1, d]])
            arrive([self.swap[2, d]])

            @pl.loop(0, 2)
            def _(k):
                add((y, k, g.c_rows(), lanes(2)), (y, k, pl.ds(0, h), lanes(2)))

            if d:
                start([self.first[2, d]])

    def s2(self):
        p, g, grad, l = self.p, self.g, self.gl_ref, self.g.l
        arrive([self.first[0, d] for d in HOPS])

        def add(gi, ref, tail):
            v = grad[gi].astype(F32)
            for k in range(3):
                v = v + ref[(k,) + tail].astype(F32)
            grad[gi] = v.astype(BF16)

        @pl.loop(0, 4)
        def _(k):
            add((k, p.xhi, g.a_rows(p.xlo), lanes(0)), self.a[0], (k,))

        start(self.second[0::3])
        arrive([self.first[1, d] for d in HOPS])

        @pl.loop(0, 4)
        def _(k):
            for j in range(2):
                add((k, j, g.b_rows(p.z), lanes(1)), self.b[0], (k, j))

        start(self.second[1::3])
        arrive([self.first[2, d] for d in HOPS])

        @pl.loop(0, 2)
        def _(k):
            add((p.y, k, g.c_rows(), lanes(2)), self.c[0], (k,))

        start(self.second[2::3])
        self.c[1][p.x] = grad[p.y, p.xhi, g.c_rows(), lanes(2)]

    def s3(self):
        p, g, grad = self.p, self.g, self.gl_ref
        arrive(self.second[0::3])
        v = grad[p.y, p.xhi, g.a_rows(p.xlo), lanes(0)].astype(F32)
        for k in range(3):
            v = v + self.a[1][k].astype(F32)
        self.a[2][p.z] = v.astype(BF16)
        start(self.third[0::3])
        arrive(self.second[1::3])
        for j in range(2):
            v = grad[p.y, j, g.b_rows(p.z), lanes(1)].astype(F32)
            for k in range(3):
                v = v + self.b[1][k, j].astype(F32)
            self.b[2][j] = v.astype(BF16)
        start(self.third[1::3])
        self.b[3][p.x] = self.b[2][p.xhi]
        arrive(self.second[2::3])
        v = self.c[1][0].astype(F32)
        for k in range(1, 4):
            v = v + self.c[1][k].astype(F32)
        self.c[2][p.z] = v.astype(BF16)
        start(self.third[2::3])

    def s4(self):
        p, g, tl = self.p, self.g, self.tl

        def total(ref):
            v = ref[0].astype(F32)
            for k in range(1, 4):
                v = v + ref[k].astype(F32)
            return v.astype(BF16)

        arrive(self.third[0::3])
        tl[g.a_rows(p.xlo), lanes(0)] = total(self.a[2])
        start(self.share_a)
        arrive(self.third[1::3])
        tl[g.b_rows(p.z), lanes(1)] = total(self.b[3])
        start(self.share_b)
        arrive(self.third[2::3])
        tl[g.c_rows(), lanes(2)] = total(self.c[2])
        start(self.share_c)

    def done(self):
        arrive(self.share_a, self.share_b, self.share_c)


FFN_ROWS = (EXPAND, 384)
ATT_ROWS = (0, 256)
N_COMM = 12


def train_kernel(count, img, cot, joint, merge, expand, reduce_w, vec_in,
                 out, dimg, total_out, g_spill, gp_spill,
                 w, sp, xs, hs, a_s, c_s, o_s, qkv, g_s, gp_s, dx_s, dzb_s, dyb_s,
                 lse_s, grad, small, total, in_stage, *rest):
    slots, (send, recv, lsem, wsem) = rest[:4 * N_COMM], rest[4 * N_COMM:]
    p = Place()
    barrier = pltpu.get_barrier_semaphore()
    friends = p.friends()

    msgs = Messages(send, recv)
    FA, FF0, F1 = (Fetch(p, Group(p, l, *rows), msgs, w)
                   for l, rows in ((0, ATT_ROWS), (0, FFN_ROWS), (1, (0, BLK))))
    RD = {}
    for n, (l, rows) in enumerate([(1, FFN_ROWS), (1, ATT_ROWS), (0, FFN_ROWS), (0, ATT_ROWS)]):
        q = slots[N_COMM * n:N_COMM * (n + 1)]
        cr = slots[N_COMM * (n % 2)]
        RD[l, rows] = Reduce(p, Group(p, l, *rows), msgs, grad, total, cr, q[1:4], q[4:8], q[8:11])

    pieces = []
    for l in range(2):
        for cb in range(3):
            pieces.append((l, joint.at[l, :, pl.ds(D * cb, D)], JOINT + 48 * cb, 48))
        pieces.append((l, merge.at[l], MERGE, 48))
        pieces.append((l, vec_in.at[l], VEC, 16))
        for cb in range(4):
            pieces.append((l, expand.at[l, :, pl.ds(D * cb, D)], EXPAND + 48 * cb, 48))
        pieces.append((l, reduce_w.at[l], REDUCE, 192))
    loads = [pltpu.make_async_copy(src, hs.at[l, pl.ds(at, n), :], wsem.at[k])
             for k, (l, src, at, n) in enumerate(pieces)]
    for cp in loads:
        cp.start()
    get_img = pltpu.make_async_copy(img, in_stage, lsem.at[3])
    get_img.start()
    for k, cp in enumerate(loads):
        cp.wait()
        if k % 10 == 9:
            l = k // 10
            for at, n in ((0, VEC + 16), (EXPAND, BLK - EXPAND)):
                w[l, p.y, p.xhi, pl.ds(at, n), :] = hs[l, pl.ds(at, n), :].astype(BF16)
            if l == 0:
                for dev in friends:
                    pl.semaphore_signal(barrier, inc=1, device_id=dev, device_id_type=MESH)
    pl.semaphore_wait(barrier, len(friends))
    FA.s1()
    FF0.s1()

    n_live = count[0]

    def rows_of(c):
        return pl.ds(pl.multiple_of(c * CH, CH), CH)

    def img_rows(i, n=R):
        return pl.ds(pl.multiple_of(i * R, R), n)

    def tail_rows(i):
        return pl.ds(pl.multiple_of(i * R, R) + 192, 16)

    get_img.wait()

    @pl.loop(0, NI)
    def _(i):
        xs[0, tail_rows(i), :] = jnp.zeros((16, D), F32)
        xs[0, img_rows(i, SEQ), :] = in_stage[i].astype(F32)

    get_cot = pltpu.make_async_copy(cot, in_stage, lsem.at[3])
    get_cot.start()
    FA.s2()
    FF0.s2()
    FA.s3()
    FF0.s3()
    FA.s4()
    FA.done()

    lane = lax.broadcasted_iota(jnp.int32, (R, 128), 1)
    row = lax.broadcasted_iota(jnp.int32, (R, 128), 0)
    mine = [lane < HD, lane >= HD]
    spare = [lane == HD, lane == 0]
    key_fill = [jnp.where(v & (row >= SEQ), -1e30, 0.0).astype(BF16) for v in spare]
    query_fill = [jnp.where(v, 1.0, 0.0).astype(BF16) for v in spare]
    blank = jnp.zeros((R, 128), BF16)
    ones = jnp.ones((16, R), BF16)

    def pieces_of(first, n):
        got, at = [], first
        while at < first + n:
            m = min(D - at % D, first + n - at)
            got.append((at // D, at % D, m))
            at += m
        return got

    def weight(l, at, first=0, n=D):
        parts = [w[l, :, :, pl.ds(at + 48 * k, 48), pl.ds(lane0, m)].reshape(D, m)
                 for k, lane0, m in pieces_of(first, n)]
        return parts[0] if len(parts) == 1 else jnp.concatenate(parts, axis=1)

    def put_grad_cols(l, at, first, val):
        done = 0
        for k, lane0, m in pieces_of(first, val.shape[1]):
            grad[l, :, :, pl.ds(at + 48 * k, 48), pl.ds(lane0, m)] = (
                val[:, done:done + m].astype(BF16).reshape(4, 2, 48, m))
            done += m

    def reduce_rows(l, first, n):
        got, at = [], first
        while at < first + n:
            m = min(192 - at % 192, first + n - at)
            s = at // 192
            got.append(w[l, s // 2, s % 2, pl.ds(REDUCE + at % 192, m), :])
            at += m
        return jnp.concatenate(got, axis=0)

    THIRDS = ((0, 512), (512, 512), (1024, 128))
    FW = 512


    plan = {}

    def during(phase, l, step, *calls):
        plan.setdefault((phase, l), {}).setdefault(step, []).extend(calls)

    def run(phase, l, n, body):
        at = plan.get((phase, l), {})

        def one(i, _):
            for step, calls in at.items():
                @pl.when(i == step)
                def _():
                    for call in calls:
                        call()
            body(i)
            return 0

        lax.fori_loop(0, n, one, 0)

    during("p1", 0, 1, FF0.s4)
    during("p2", 0, 1, F1.s1)
    during("p3", 0, 0, F1.s2, F1.s3)
    during("p3", 0, 1, F1.s4)

    spills = [(g_s, g_spill, lsem.at[4]), (gp_s, gp_spill, lsem.at[5])]

    for l in range(2):
        if l:
            F1.done()
        acc = w[l, 0, 0, pl.ds(VEC, 16), :].astype(F32)
        for s in range(1, 8):
            acc = acc + w[l, s // 2, s % 2, pl.ds(VEC, 16), :].astype(F32)
        sp[l] = acc
        vec = lambda r: sp[l, r:r + 1, :]

        def p1(c):
            rows = rows_of(c)
            xhat, _r = normalize(xs[l, rows, :])
            a = (xhat * vec(0) + vec(1)).astype(BF16)
            a_s[l, rows, :] = a
            for first, n in THIRDS:
                val = dot(a, weight(l, JOINT, first, n))
                if first == 0:
                    val = jnp.concatenate([val[:, :D] * (HD ** -0.5), val[:, D:]], axis=1)
                qkv[l, rows, pl.ds(first, n)] = val.astype(BF16)

        run("p1", l, NCH, p1)

        def p2(k):
            heads = [(2 * k + u, j, e) for u in range(2) for j in range(3) for e in range(2)]
            scores, tops, weights, parts = [], [], [], []
            for i, j, e in heads:
                rows = img_rows(i)
                q2 = qkv[l, rows, pl.ds(128 * j, 128)]
                k2 = qkv[l, rows, pl.ds(D + 128 * j, 128)]
                scores.append(dot_nt(jnp.where(mine[e], k2, key_fill[e]),
                                     jnp.where(mine[e], q2, query_fill[e])))
            for st in scores:
                tops.append(jnp.max(st, axis=0, keepdims=True))
                weights.append(jnp.exp(st - tops[-1]).astype(BF16))
            for n, (i, j, e) in enumerate(heads):
                rows = img_rows(i)
                if e == 0:
                    v2t = qkv[l, rows, pl.ds(2 * D + 128 * j, 128)].T
                val = dot(jnp.concatenate([v2t[HD * e:HD * (e + 1), :], ones], axis=0), weights[n])
                tot = val[HD:HD + 1, :]
                lse_s[l, i, 2 * j + e:2 * j + e + 1, :] = tops[n] + jnp.log(tot)
                parts.append(val[:HD, :] * (1.0 / tot))
                if e == 1:
                    o_s[l, rows, pl.ds(128 * j, 128)] = jnp.concatenate(parts[-2:], axis=0).T.astype(BF16)

        run("p2", l, NI // 2, p2)

        if l == 0:
            FF0.done()
        else:
            for src, dst, sem in spills:
                pltpu.make_async_copy(src, dst, sem).wait()

        def p3(c):
            rows = rows_of(c)
            h = xs[l, rows, :] + dot(o_s[l, rows, :], weight(l, MERGE))
            hs[l, rows, :] = h
            xhat, _r = normalize(h)
            cc = (xhat * vec(2) + vec(3)).astype(BF16)
            c_s[l, rows, :] = cc
            acc = h + vec(4)
            bias = jnp.concatenate([vec(5 + k) for k in range(4)], axis=1)
            u, g = {}, {}
            for f in range(FF // FW + 2):
                if f < FF // FW:
                    u[f] = dot(cc, weight(l, EXPAND, FW * f, FW)) + bias[:, FW * f:FW * (f + 1)]
                if 1 <= f <= FF // FW:
                    val, slope = gelu_pair(u[f - 1])
                    g[f - 1] = val.astype(BF16)
                    g_s[rows, pl.ds(FW * (f - 1), FW)] = g[f - 1]
                    gp_s[rows, pl.ds(FW * (f - 1), FW)] = slope.astype(BF16)
                if f >= 2:
                    acc = acc + dot(g[f - 2], reduce_rows(l, FW * (f - 2), FW))
            if l == 0:
                xs[1, rows, :] = acc
            else:
                for k in range(CH // R):
                    i = c * (CH // R) + k
                    live = jnp.where(i < n_live, 1.0, 0.0).astype(F32)
                    dx_s[img_rows(i), :] = acc[R * k:R * (k + 1), :] * live

        run("p3", l, NCH, p3)
        if l == 0:
            for src, dst, sem in spills:
                pltpu.make_async_copy(src, dst, sem).start()

    put_out = pltpu.make_async_copy(dx_s, out, lsem.at[6])
    put_out.start()
    small[...] = jnp.zeros_like(small)
    get_cot.wait()
    put_out.wait()

    @pl.loop(0, NI)
    def _(i):
        live = jnp.where(i < n_live, 1.0, 0.0).astype(F32)
        dx_s[tail_rows(i), :] = jnp.zeros((16, D), F32)
        dx_s[img_rows(i, SEQ), :] = in_stage[i].astype(F32) * live

    R1, R2, R3, R4 = RD[1, FFN_ROWS], RD[1, ATT_ROWS], RD[0, FFN_ROWS], RD[0, ATT_ROWS]
    during("b2", 1, 2, R1.s1)
    during("b3", 1, 0, R1.s2)
    during("b1", 0, 0, R1.s3)
    during("b1", 0, 1, R1.s4, R2.s1)
    during("b2", 0, 0, R2.s2)
    during("b2", 0, 2, R3.s1)
    during("b2", 0, 3, R2.s3)
    during("b2", 0, 5, R2.s4)
    during("b3", 0, 0, R3.s2)
    during("b3", 0, 1, R3.s3)

    def colsum(v):
        return jnp.sum(v, axis=0, keepdims=True)

    for l in (1, 0):
        vec = lambda r: sp[l, r:r + 1, :]
        if l == 0:
            for dst, src, sem in spills:
                pltpu.make_async_copy(src, dst, sem).wait()

        def b1(c):
            rows = rows_of(c)
            dx = dx_s[rows, :]
            dzb = dx.astype(BF16)
            dzb_s[rows, :] = dzb
            small[l, 4:5, :] += colsum(dzb.astype(F32))
            dg = {}
            for f in range(FF // FW + 1):
                if f < FF // FW:
                    dg[f] = dot_nt(dzb, reduce_rows(l, FW * f, FW))
                if f >= 1:
                    at = pl.ds(FW * (f - 1), FW)
                    gp_s[rows, at] = (dg[f - 1] * gp_s[rows, at].astype(F32)).astype(BF16)
            for k in range(4):
                small[l, 5 + k:6 + k, :] += colsum(gp_s[rows, pl.ds(D * k, D)].astype(F32))
            dc = dot_nt(gp_s[rows, :], weight(l, EXPAND, 0, FF))
            xhat, rstd = normalize(hs[l, rows, :])
            small[l, 2:3, :] += colsum(dc * xhat)
            small[l, 3:4, :] += colsum(dc)
            dh = dx + norm_back(dc, xhat, rstd, vec(2))
            dx_s[rows, :] = dh
            dyb = dh.astype(BF16)
            dyb_s[rows, :] = dyb
            hs[l, rows, :] = dot_nt(dyb, weight(l, MERGE))

        run("b1", l, NCH, b1)

        for f in range(FF // FW):
            put_grad_cols(l, EXPAND, FW * f, dot_tn(c_s[l], gp_s[:, pl.ds(FW * f, FW)]))
        for f in (0, 2):
            val = dot_tn(dzb_s[...], g_s[:, pl.ds(D * f, 2 * D)])
            grad[l, f, :, pl.ds(REDUCE, 192), :] = val[:, :D].T.astype(BF16).reshape(2, 192, D)
            grad[l, f + 1, :, pl.ds(REDUCE, 192), :] = val[:, D:].T.astype(BF16).reshape(2, 192, D)
        RD[l, FFN_ROWS].begin()
        if l:
            for dst, src, sem in spills:
                pltpu.make_async_copy(src, dst, sem).start()
        put_grad_cols(l, MERGE, 0, dot_tn(o_s[l], dyb_s[...]))

        def b2(i):
            rows = img_rows(i)
            heads = [(j, e) for j in range(3) for e in range(2)]
            scores, slopes, weights, down_scores = [], [], [], []
            dq, dk, dv, down = [], [], [], []
            for j, e in heads:
                q2 = qkv[l, rows, pl.ds(128 * j, 128)]
                k2 = qkv[l, rows, pl.ds(D + 128 * j, 128)]
                v2 = qkv[l, rows, pl.ds(2 * D + 128 * j, 128)]
                do2 = hs[l, rows, pl.ds(128 * j, 128)].astype(BF16)
                down.append(do2)
                scores.append(dot_nt(jnp.where(mine[e], k2, key_fill[e]),
                                     jnp.where(mine[e], q2, query_fill[e])))
                slopes.append(dot_nt(v2, jnp.where(mine[e], do2, blank)))
            for n, (j, e) in enumerate(heads):
                pt = jnp.exp(scores[n] - lse_s[l, i, n:n + 1, :])
                r = jnp.sum(slopes[n] * pt, axis=0, keepdims=True)
                weights.append(pt.astype(BF16))
                down_scores.append((pt * (slopes[n] - r)).astype(BF16))
            for n, (j, e) in enumerate(heads):
                if e == 0:
                    k2t = qkv[l, rows, pl.ds(D + 128 * j, 128)].T
                dv.append(dot(weights[n], down[n]))
                dk.append(dot(down_scores[n], qkv[l, rows, pl.ds(128 * j, 128)]))
                dq.append(dot(k2t[HD * e:HD * (e + 1), :], down_scores[n]))
                if e == 1:
                    new_q = jnp.concatenate(dq[-2:], axis=0).T * (HD ** -0.5)
                    qkv[l, rows, pl.ds(128 * j, 128)] = new_q.astype(BF16)
                    qkv[l, rows, pl.ds(D + 128 * j, 128)] = jnp.where(mine[0], *dk[-2:]).astype(BF16)
                    qkv[l, rows, pl.ds(2 * D + 128 * j, 128)] = jnp.where(mine[0], *dv[-2:]).astype(BF16)

        run("b2", l, NI, b2)

        def b3(c):
            rows = rows_of(c)
            da = dot_nt(qkv[l, rows, :], weight(l, JOINT, 0, 3 * D))
            xhat, rstd = normalize(xs[l, rows, :])
            small[l, 0:1, :] += colsum(da * xhat)
            small[l, 1:2, :] += colsum(da)
            dx = dx_s[rows, :] + norm_back(da, xhat, rstd, vec(0))
            dx_s[rows, :] = dx

        run("b3", l, NCH, b3)

        for s in range(8):
            grad[l, s // 2, s % 2, pl.ds(VEC, 16), :] = small[l].astype(BF16)
        for first, n in THIRDS:
            put_grad_cols(l, JOINT, first, dot_tn(a_s[l], qkv[l, :, pl.ds(first, n)]))
        RD[l, ATT_ROWS].begin()

    put_grad = pltpu.make_async_copy(dx_s, dimg, lsem.at[6])
    put_grad.start()
    R3.s4()
    R4.s1()
    R4.s2()
    for build in msgs.made[:3 * 29]:
        build().wait_send()
    R4.s3()
    R4.s4()
    for rd in (R1, R2, R3, R4):
        rd.done()
    put_total = pltpu.make_async_copy(total, total_out, lsem.at[7])
    put_total.start()
    for build in msgs.made[3 * 29:]:
        build().wait_send()
    put_grad.wait()
    put_total.wait()


def train(count, img, cot, joint, merge, expand, reduce_w, vec):
    A = pl.BlockSpec(memory_space=pl.ANY)
    vm = lambda *shape: pltpu.VMEM(shape, BF16)
    vf = lambda *shape: pltpu.VMEM(shape, F32)
    slots = []
    for k, n in enumerate((384, 256, 384, 256)):
        n4, n8, h = n // 4, n // 8, n // 2
        slots += [vm(4, 2, h, D) if k < 2 else vm(16, 128),
                  vm(3, 4, n4, 128), vm(3, n4, 128), vm(4, n4, 128),
                  vm(3, 4, 2, n8, 128), vm(3, 2, n8, 128), vm(2, n8, 128), vm(4, n8, 128),
                  vm(3, 2, h, 128), vm(4, h, 128), vm(4, h, 128), vm(16, 128)]
    return pl.pallas_call(
        train_kernel,
        out_shape=(
            jax.ShapeDtypeStruct((T, D), F32),
            jax.ShapeDtypeStruct((T, D), F32),
            jax.ShapeDtypeStruct((2, BLK, D), BF16),
            jax.ShapeDtypeStruct((T, FF), BF16),
            jax.ShapeDtypeStruct((T, FF), BF16),
        ),
        in_specs=[pl.BlockSpec(memory_space=pltpu.SMEM)] + [A] * 7,
        out_specs=(A,) * 5,
        scratch_shapes=[
            vm(2, 4, 2, BLK, D), vf(2, 16, D),
            vf(2, T, D), vf(2, T, D),
            vm(2, T, D), vm(2, T, D), vm(2, T, D),
            vm(2, T, 3 * D), vm(T, FF), vm(T, FF),
            vf(T, D), vm(T, D), vm(T, D),
            vf(2, NI, 8, R),
            vm(2, 4, 2, BLK, D), vf(2, 16, D), vm(2, BLK, D),
            vm(NI, SEQ, D),
            *slots,
            pltpu.SemaphoreType.DMA((N_SEMS,)), pltpu.SemaphoreType.DMA((N_SEMS,)),
            pltpu.SemaphoreType.DMA((8,)), pltpu.SemaphoreType.DMA((20,)),
        ],
        compiler_params=pltpu.CompilerParams(collective_id=0, has_side_effects=True,
                                             vmem_limit_bytes=65200 * 1024),
        cost_estimate=pl.CostEstimate(flops=28_000_000_000, bytes_accessed=20_000_000,
                                      transcendentals=8_000_000),
    )(count, img, cot, joint, merge, expand, reduce_w, vec)


N_SEMS = 3 * 29 + 4 * 50


BETA_ONE = 0.9
BETA_TWO = 0.999
ADAM_EPS = 1e-08
DECAY_MATRIX = 0.05
RATE_MATRIX = 0.05
RATE_SMALL = 0.4
STEP = 10


def adam_update(gradient, first_moment, second_moment, master, step_rate, decay_rate):
    first_new = BETA_ONE * first_moment + (1.0 - BETA_ONE) * gradient
    second_new = BETA_TWO * second_moment + (1.0 - BETA_TWO) * gradient * gradient
    corrected = first_new / (1.0 - BETA_ONE**STEP)
    denominator = jnp.sqrt(second_new / (1.0 - BETA_TWO**STEP)) + ADAM_EPS
    master_new = master - step_rate * (corrected / denominator + decay_rate * master)
    return (first_new, second_new, master_new)


def adam_kernel(g, rows_a, rows_b, *refs):
    ins, outs = refs[:12], refs[12:28]
    for src, dst in ((rows_a, refs[28]), (rows_b, refs[29])):
        dst[...] = src[:, :SEQ, :]
    for kind, (at, blocks, rows) in enumerate(
            [(JOINT, 3, 48), (MERGE, 1, 48), (EXPAND, 4, 48), (REDUCE, 1, 192)]):
        for cb in range(blocks):
            grad = g[0, pl.ds(at + 48 * cb, rows), :].astype(F32)
            cols = (0, slice(None), pl.ds(D * cb, D))
            m, v, wt = (ins[3 * kind + k][cols] for k in range(3))
            new = adam_update(grad, m, v, wt, RATE_MATRIX, DECAY_MATRIX)
            for k, val in enumerate((grad,) + new):
                outs[4 * kind + k][cols] = val


def adam(g, padded, firsts, seconds, masters):
    widths = (3 * D, D, 4 * D, D)
    rows = (48, 48, 48, 192)
    spec = [pl.BlockSpec((1, r, wd), lambda l: (l, 0, 0)) for r, wd in zip(rows, widths)]
    ins, in_specs, out_specs, shapes = [], [], [], []
    for k in range(4):
        for a in (firsts[k], seconds[k], masters[k]):
            ins.append(a)
            in_specs.append(spec[k])
        for _ in range(4):
            out_specs.append(spec[k])
            shapes.append(jax.ShapeDtypeStruct(masters[k].shape, F32))
    for _ in range(2):
        out_specs.append(pl.BlockSpec((NI // 2, SEQ, D), lambda l: (l, 0, 0)))
        shapes.append(jax.ShapeDtypeStruct((NI, SEQ, D), F32))
    return pl.pallas_call(
        adam_kernel,
        grid=(2,),
        out_shape=tuple(shapes),
        in_specs=[pl.BlockSpec((1, BLK, D), lambda l: (l, 0, 0))]
        + [pl.BlockSpec((NI // 2, R, D), lambda l: (l, 0, 0))] * 2 + in_specs,
        out_specs=tuple(out_specs),
        compiler_params=pltpu.CompilerParams(vmem_limit_bytes=32 * 1024 * 1024),
    )(g, *padded, *ins)


def shards(images, cotangent, image_count, joint_weight, merge_weight, expand_weight,
           reduce_weight, small_params, joint_first, merge_first, expand_first, reduce_first,
           small_first, joint_second, merge_second, expand_second, reduce_second, small_second):
    masters = (joint_weight, merge_weight, expand_weight, reduce_weight)
    firsts = (joint_first, merge_first, expand_first, reduce_first)
    seconds = (joint_second, merge_second, expand_second, reduce_second)
    width = small_params.shape[1]
    rank = lax.axis_index("shard")
    vec = lax.dynamic_update_slice_in_dim(jnp.zeros((2, 16 * D), F32), small_params, rank * width, 1)
    block_out, image_grad, total, _g, _gp = train(
        image_count, images, cotangent, *masters, vec.reshape(2, 16, D))
    done = adam(total, [v.reshape(NI, R, D) for v in (block_out, image_grad)], firsts, seconds, masters)
    vec_grad = lax.dynamic_slice_in_dim(total[:, VEC:VEC + 9].reshape(2, 9 * D), rank * width, width, 1)
    vec_grad = vec_grad.astype(F32)
    vec_done = (vec_grad,) + adam_update(vec_grad, small_first, small_second, small_params,
                                         RATE_SMALL, 0.0)
    outputs = list(done[16:])
    for member in range(4):
        outputs += [done[4 * kind + member] for kind in range(4)] + [vec_done[member]]
    return tuple(outputs)


def solution(mesh):
    whole = P(("replica", "shard"), None, None)
    weights = [P(None, "shard", None)] * 4 + [P(None, "shard")]
    return jax.shard_map(
        shards,
        mesh=mesh,
        in_specs=(whole, whole, P(("replica", "shard"))) + tuple(weights * 3),
        out_specs=(whole, whole) + tuple(weights * 4),
        check_vma=False,
    )
```

```python
import jax
import jax.numpy as jnp
from jax import lax
from jax.experimental import pallas as pl
from jax.experimental.pallas import tpu as pltpu
from jax.sharding import PartitionSpec as P

D = 384
FF = 1536
HD = 64
NI = 6
SEQ = 197
R = 208
T = NI * R
CH = 624
NCH = T // CH
BLK = 640
JOINT, MERGE, VEC, EXPAND, REDUCE = 0, 144, 192, 256, 448
NORM_EPS = 1e-6
F32 = jnp.float32
BF16 = jnp.bfloat16
MESH = pl.DeviceIdType.MESH
HOPS = (1, 3, 2)


def dot(a, b):
    return lax.dot_general(a, b, (((1,), (0,)), ((), ())), preferred_element_type=F32)


def dot_nt(a, b):
    return lax.dot_general(a, b, (((1,), (1,)), ((), ())), preferred_element_type=F32)


def dot_tn(a, b):
    return lax.dot_general(a, b, (((0,), (0,)), ((), ())), preferred_element_type=F32)


def normalize(v):
    centered = v - jnp.mean(v, axis=-1, keepdims=True)
    variance = jnp.mean(centered * centered, axis=-1, keepdims=True)
    rstd = lax.rsqrt(variance + NORM_EPS)
    return centered * rstd, rstd


def gelu_pair(u):
    z = jnp.abs(u)
    d = 1.0 + (0.3275911 * 0.7071067811865476) * z
    t = 1.0 / d
    e = jnp.exp(-0.5 * (u * u))
    poly = ((((0.5 * 1.061405429) * t - 0.5 * 1.453152027) * t + 0.5 * 1.421413741) * t
            - 0.5 * 0.284496736) * t + 0.5 * 0.254829592
    half = poly * t * e
    phi = jnp.where(u < 0, half, 1.0 - half)
    return u * phi, phi + u * (e * 0.3989422804014327)


def norm_back(dy, xhat, rstd, gain):
    dxh = dy * gain
    m1 = jnp.mean(dxh, axis=-1, keepdims=True)
    m2 = jnp.mean(dxh * xhat, axis=-1, keepdims=True)
    return rstd * (dxh - m1 - xhat * m2)


class Place:
    def __init__(self):
        r = lax.axis_index("replica")
        s = lax.axis_index("shard")
        self.c = lax.rem(r, 2)
        self.xlo = lax.rem(lax.div(r, 2), 2)
        self.z = lax.div(r, 4)
        self.xhi = lax.rem(s, 2)
        self.y = lax.div(s, 2)
        self.x = self.xhi * 2 + self.xlo
        self.twin = self.xhi * 2 + 1 - self.xlo

    def at(self, **change):
        q = dict(x=self.x, y=self.y, z=self.z, c=self.c, **{})
        q.update(change)
        return (q["z"] * 4 + lax.rem(q["x"], 2) * 2 + q["c"], q["y"] * 2 + lax.div(q["x"], 2))

    def step(self, axis, d):
        return lax.rem(getattr(self, axis) + d, 4)

    def partner(self):
        return self.at(c=1 - self.c)

    def across(self):
        return self.at(x=3 - self.x)

    def friends(self):
        other = 1 - self.c
        return ([self.partner(), self.at(x=self.twin, c=other)]
                + [self.at(**{a: self.step(a, d)}) for a in "xyz" for d in HOPS]
                + [self.at(z=self.step("z", d), c=other) for d in HOPS])


def lanes(t):
    return pl.ds(128 * t, 128)


def span(start, n):
    return pl.ds(pl.multiple_of(start, 16), n)


class Group:
    def __init__(self, p, l, g0, n):
        self.p, self.l, self.g0, self.n, self.h = p, l, g0, n, n // 2

    def a_rows(self, xlo, c=None):
        return span(self.base(c) + xlo * (self.n // 4), self.n // 4)

    def b_rows(self, z, c=None):
        return span(self.base(c) + z * (self.n // 8), self.n // 8)

    def c_rows(self, c=None):
        return span(self.base(c), self.h)

    def base(self, c=None):
        return self.g0 + (self.p.c if c is None else c) * self.h


class Messages:
    def __init__(self, send, recv):
        self.send, self.recv, self.n, self.made = send, recv, 0, []

    def new(self, src, dst, dev):
        k = self.n
        self.n += 1

        def build():
            return pltpu.make_async_remote_copy(
                src_ref=src(), dst_ref=dst(), send_sem=self.send.at[k], recv_sem=self.recv.at[k],
                device_id=dev(), device_id_type=MESH)

        self.made.append(build)
        return build


def start(*groups):
    for group in groups:
        for build in group:
            build().start()


def arrive(*groups):
    for group in groups:
        for build in group:
            build().wait_recv()


class Fetch:
    def __init__(self, p, g, msgs, w):
        self.g = g
        wl = w.at[g.l]
        s = slice(None)
        ra, rb, rc = (lambda v=None: g.a_rows(p.xlo if v is None else v),
                      lambda v=None: g.b_rows(p.z if v is None else v), lambda: g.c_rows())
        ha = lambda: wl.at[p.y, p.xhi, ra(), lanes(0)]
        hb = lambda: wl.at[p.y, p.xhi, rb(), lanes(1)]
        hc = lambda: wl.at[p.y, p.xhi, rc(), lanes(2)]
        ydev = lambda d: (lambda: p.at(y=p.step("y", d)))
        xdev = lambda d: (lambda: p.at(x=p.step("x", d)))
        zdev = lambda d: (lambda: p.at(z=p.step("z", d)))
        self.c1 = [msgs.new(hc, hc, p.across)]
        self.a1 = [msgs.new(ha, ha, ydev(d)) for d in HOPS]
        self.b1 = [msgs.new(hb, hb, ydev(d)) for d in HOPS]
        ax = lambda x: (lambda: wl.at[s, lax.div(x(), 2), ra(lax.rem(x(), 2)), lanes(0)])
        cy = lambda y: (lambda: wl.at[y(), s, rc(), lanes(2)])
        bz = lambda z: (lambda: wl.at[s, s, rb(z()), lanes(1)])
        bx = lambda: wl.at[s, p.xhi, rb(), lanes(1)]
        x0, y0, z0 = (lambda: p.x), (lambda: p.y), (lambda: p.z)
        self.a2 = [msgs.new(ax(x0), ax(x0), xdev(d)) for d in HOPS]
        self.c2 = [msgs.new(cy(y0), cy(y0), ydev(d)) for d in HOPS]
        self.b2 = [msgs.new(bx, bx, p.across)]
        self.b3 = [msgs.new(bz(z0), bz(z0), zdev(d)) for d in HOPS]
        fw = lambda r: msgs.new(r, r, p.partner)
        back = lambda axis, d: (lambda: p.step(axis, (4 - d) % 4))
        self.fa = [fw(ax(back("x", d))) for d in (0,) + HOPS]
        self.fb = [fw(bz(back("z", d))) for d in (0,) + HOPS]
        self.fc = [fw(cy(back("y", d))) for d in (0,) + HOPS]

    def s1(self):
        start(self.c1, self.a1, self.b1)

    def s2(self):
        arrive(self.c1)
        start(self.c2)
        arrive(self.b1)
        start(self.b2)
        arrive(self.a1)
        start(self.a2, self.fa[:1])

    def s3(self):
        arrive(self.b2)
        start(self.b3, self.fb[:1], self.fc[:1])

    def s4(self):
        for k in range(3):
            for got, pass_on in ((self.c2, self.fc), (self.a2, self.fa), (self.b3, self.fb)):
                arrive(got[k:k + 1])
                start(pass_on[k + 1:k + 2])

    def done(self):
        arrive(self.fa, self.fb, self.fc)


class Reduce:
    def __init__(self, p, g, msgs, grad, total, cr, a, b, c):
        self.p, self.g = p, g
        s = slice(None)
        n4, n8, h = g.n // 4, g.n // 8, g.h
        gl = grad.at[g.l]
        tl = total.at[g.l]
        self.gl_ref, self.tl, self.cr = gl, tl, cr
        self.a, self.b, self.c = a, b, c
        hi, lo = (lambda v: lax.div(v, 2)), (lambda v: lax.rem(v, 2))
        go = lambda axis, d: (lambda: p.step(axis, d))
        dev = lambda axis, d: (lambda: p.at(**{axis: p.step(axis, d)}))
        other = lambda: 1 - p.c
        self.swap = {}
        for d in HOPS + (0,):
            x, y, z = go("x", d), go("y", d), go("z", d)
            self.swap[0, d] = msgs.new(
                lambda x=x: gl.at[s, hi(x()), g.a_rows(lo(x()), other()), lanes(0)],
                lambda x=x: cr.at[s, hi(x()), span(lo(x()) * n4, n4), lanes(0)], p.partner)
            self.swap[1, d] = msgs.new(
                lambda z=z: gl.at[s, s, g.b_rows(z(), other()), lanes(1)],
                lambda z=z: cr.at[s, s, span(z() * n8, n8), lanes(1)], p.partner)
            self.swap[2, d] = msgs.new(
                lambda y=y: gl.at[y(), s, g.c_rows(other()), lanes(2)],
                lambda y=y: cr.at[y(), s, pl.ds(0, h), lanes(2)], p.partner)
        self.first = {}
        for d in HOPS:
            x, y, z = go("x", d), go("y", d), go("z", d)
            self.first[0, d] = msgs.new(
                lambda x=x: gl.at[s, hi(x()), g.a_rows(lo(x())), lanes(0)],
                lambda d=d: a[0].at[d - 1], dev("x", d))
            self.first[1, d] = msgs.new(
                lambda z=z: gl.at[s, s, g.b_rows(z()), lanes(1)],
                lambda d=d: b[0].at[d - 1], dev("z", d))
            self.first[2, d] = msgs.new(
                lambda y=y: gl.at[y(), s, g.c_rows(), lanes(2)],
                lambda d=d: c[0].at[d - 1], dev("y", d))
        self.second = []
        self.third = []
        for d in HOPS:
            x, y = go("x", d), go("y", d)
            self.second.append(msgs.new(
                lambda y=y: gl.at[y(), p.xhi, g.a_rows(p.xlo), lanes(0)],
                lambda d=d: a[1].at[d - 1], dev("y", d)))
            self.second.append(msgs.new(
                lambda y=y: gl.at[y(), s, g.b_rows(p.z), lanes(1)],
                lambda d=d: b[1].at[d - 1], dev("y", d)))
            self.second.append(msgs.new(
                lambda x=x: gl.at[p.y, hi(x()), g.c_rows(), lanes(2)],
                lambda: c[1].at[p.x], dev("x", d)))
            self.third.append(msgs.new(lambda: a[2].at[p.z], lambda: a[2].at[p.z], dev("z", d)))
            self.third.append(msgs.new(lambda x=x: b[2].at[hi(x())], lambda: b[3].at[p.x], dev("x", d)))
            self.third.append(msgs.new(lambda: c[2].at[p.z], lambda: c[2].at[p.z], dev("z", d)))
        ra = lambda: tl.at[g.a_rows(p.xlo), lanes(0)]
        rb = lambda: tl.at[g.b_rows(p.z), lanes(1)]
        rc = lambda: tl.at[g.c_rows(), lanes(2)]
        self.share_a = [msgs.new(ra, ra, lambda: p.at(x=p.twin)),
                        msgs.new(ra, ra, lambda: p.at(x=p.twin, c=1 - p.c)),
                        msgs.new(ra, ra, p.partner)]
        self.share_b = [msgs.new(rb, rb, p.partner)]
        for d in HOPS:
            self.share_b.append(msgs.new(rb, rb, dev("z", d)))
            self.share_b.append(msgs.new(rb, rb, lambda d=d: p.at(z=p.step("z", d), c=1 - p.c)))
        self.share_c = [msgs.new(rc, rc, p.partner)]

    def begin(self):
        for d in HOPS + (0,):
            start([self.swap[t, d] for t in range(3)])

    def s1(self):
        p, g, grad, cr, l = self.p, self.g, self.gl_ref, self.cr, self.g.l
        n4, n8, h = g.n // 4, g.n // 8, g.h

        def add(gi, ci):
            grad[gi] = (grad[gi].astype(F32) + cr[ci].astype(F32)).astype(BF16)

        for d in HOPS + (0,):
            x, y, z = p.step("x", d), p.step("y", d), p.step("z", d)
            arrive([self.swap[0, d]])

            @pl.loop(0, 4)
            def _(k):
                add((k, lax.div(x, 2), g.a_rows(lax.rem(x, 2)), lanes(0)),
                    (k, lax.div(x, 2), span(lax.rem(x, 2) * n4, n4), lanes(0)))

            if d:
                start([self.first[0, d]])
            arrive([self.swap[1, d]])

            @pl.loop(0, 4)
            def _(k):
                for j in range(2):
                    add((k, j, g.b_rows(z), lanes(1)), (k, j, span(z * n8, n8), lanes(1)))

            if d:
                start([self.first[1, d]])
            arrive([self.swap[2, d]])

            @pl.loop(0, 2)
            def _(k):
                add((y, k, g.c_rows(), lanes(2)), (y, k, pl.ds(0, h), lanes(2)))

            if d:
                start([self.first[2, d]])

    def s2(self):
        p, g, grad, l = self.p, self.g, self.gl_ref, self.g.l
        arrive([self.first[0, d] for d in HOPS])

        def add(gi, ref, tail):
            v = grad[gi].astype(F32)
            for k in range(3):
                v = v + ref[(k,) + tail].astype(F32)
            grad[gi] = v.astype(BF16)

        @pl.loop(0, 4)
        def _(k):
            add((k, p.xhi, g.a_rows(p.xlo), lanes(0)), self.a[0], (k,))

        start(self.second[0::3])
        arrive([self.first[1, d] for d in HOPS])

        @pl.loop(0, 4)
        def _(k):
            for j in range(2):
                add((k, j, g.b_rows(p.z), lanes(1)), self.b[0], (k, j))

        start(self.second[1::3])
        arrive([self.first[2, d] for d in HOPS])

        @pl.loop(0, 2)
        def _(k):
            add((p.y, k, g.c_rows(), lanes(2)), self.c[0], (k,))

        start(self.second[2::3])
        self.c[1][p.x] = grad[p.y, p.xhi, g.c_rows(), lanes(2)]

    def s3(self):
        p, g, grad = self.p, self.g, self.gl_ref
        arrive(self.second[0::3])
        v = grad[p.y, p.xhi, g.a_rows(p.xlo), lanes(0)].astype(F32)
        for k in range(3):
            v = v + self.a[1][k].astype(F32)
        self.a[2][p.z] = v.astype(BF16)
        start(self.third[0::3])
        arrive(self.second[1::3])
        for j in range(2):
            v = grad[p.y, j, g.b_rows(p.z), lanes(1)].astype(F32)
            for k in range(3):
                v = v + self.b[1][k, j].astype(F32)
            self.b[2][j] = v.astype(BF16)
        start(self.third[1::3])
        self.b[3][p.x] = self.b[2][p.xhi]
        arrive(self.second[2::3])
        v = self.c[1][0].astype(F32)
        for k in range(1, 4):
            v = v + self.c[1][k].astype(F32)
        self.c[2][p.z] = v.astype(BF16)
        start(self.third[2::3])

    def s4(self):
        p, g, tl = self.p, self.g, self.tl

        def total(ref):
            v = ref[0].astype(F32)
            for k in range(1, 4):
                v = v + ref[k].astype(F32)
            return v.astype(BF16)

        arrive(self.third[0::3])
        tl[g.a_rows(p.xlo), lanes(0)] = total(self.a[2])
        start(self.share_a)
        arrive(self.third[1::3])
        tl[g.b_rows(p.z), lanes(1)] = total(self.b[3])
        start(self.share_b)
        arrive(self.third[2::3])
        tl[g.c_rows(), lanes(2)] = total(self.c[2])
        start(self.share_c)

    def done(self):
        arrive(self.share_a, self.share_b, self.share_c)


FFN_ROWS = (EXPAND, 384)
ATT_ROWS = (0, 256)
N_COMM = 12


def train_kernel(count, img, cot, joint, merge, expand, reduce_w, vec_in,
                 out, dimg, total_out, g_spill, gp_spill,
                 w, sp, xs, hs, a_s, c_s, o_s, qkv, g_s, gp_s, dx_s, dzb_s, dyb_s,
                 lse_s, grad, small, total, in_stage, *rest):
    slots, (send, recv, lsem, wsem) = rest[:4 * N_COMM], rest[4 * N_COMM:]
    p = Place()
    barrier = pltpu.get_barrier_semaphore()
    friends = p.friends()

    msgs = Messages(send, recv)
    FA, FF0, F1 = (Fetch(p, Group(p, l, *rows), msgs, w)
                   for l, rows in ((0, ATT_ROWS), (0, FFN_ROWS), (1, (0, BLK))))
    RD = {}
    for n, (l, rows) in enumerate([(1, FFN_ROWS), (1, ATT_ROWS), (0, FFN_ROWS), (0, ATT_ROWS)]):
        q = slots[N_COMM * n:N_COMM * (n + 1)]
        cr = slots[N_COMM * (n % 2)]
        RD[l, rows] = Reduce(p, Group(p, l, *rows), msgs, grad, total, cr, q[1:4], q[4:8], q[8:11])

    pieces = []
    for l in range(2):
        for cb in range(3):
            pieces.append((l, joint.at[l, :, pl.ds(D * cb, D)], JOINT + 48 * cb, 48))
        pieces.append((l, merge.at[l], MERGE, 48))
        pieces.append((l, vec_in.at[l], VEC, 16))
        for cb in range(4):
            pieces.append((l, expand.at[l, :, pl.ds(D * cb, D)], EXPAND + 48 * cb, 48))
        pieces.append((l, reduce_w.at[l], REDUCE, 192))
    loads = [pltpu.make_async_copy(src, hs.at[l, pl.ds(at, n), :], wsem.at[k])
             for k, (l, src, at, n) in enumerate(pieces)]
    for cp in loads:
        cp.start()
    get_img = pltpu.make_async_copy(img, in_stage, lsem.at[3])
    get_img.start()
    for k, cp in enumerate(loads):
        cp.wait()
        if k % 10 == 9:
            l = k // 10
            for at, n in ((0, VEC + 16), (EXPAND, BLK - EXPAND)):
                w[l, p.y, p.xhi, pl.ds(at, n), :] = hs[l, pl.ds(at, n), :].astype(BF16)
            if l == 0:
                for dev in friends:
                    pl.semaphore_signal(barrier, inc=1, device_id=dev, device_id_type=MESH)
    pl.semaphore_wait(barrier, len(friends))
    FA.s1()
    FF0.s1()

    n_live = count[0]

    def rows_of(c):
        return pl.ds(pl.multiple_of(c * CH, CH), CH)

    def img_rows(i, n=R):
        return pl.ds(pl.multiple_of(i * R, R), n)

    def tail_rows(i):
        return pl.ds(pl.multiple_of(i * R, R) + 192, 16)

    get_img.wait()

    @pl.loop(0, NI)
    def _(i):
        xs[0, tail_rows(i), :] = jnp.zeros((16, D), F32)
        xs[0, img_rows(i, SEQ), :] = in_stage[i].astype(F32)

    get_cot = pltpu.make_async_copy(cot, in_stage, lsem.at[3])
    get_cot.start()
    FA.s2()
    FF0.s2()
    FA.s3()
    FF0.s3()
    FA.s4()
    FA.done()

    lane = lax.broadcasted_iota(jnp.int32, (R, 128), 1)
    row = lax.broadcasted_iota(jnp.int32, (R, 128), 0)
    mine = [lane < HD, lane >= HD]
    spare = [lane == HD, lane == 0]
    key_fill = [jnp.where(v & (row >= SEQ), -1e30, 0.0).astype(BF16) for v in spare]
    query_fill = [jnp.where(v, 1.0, 0.0).astype(BF16) for v in spare]
    blank = jnp.zeros((R, 128), BF16)
    ones = jnp.ones((16, R), BF16)

    def pieces_of(first, n):
        got, at = [], first
        while at < first + n:
            m = min(D - at % D, first + n - at)
            got.append((at // D, at % D, m))
            at += m
        return got

    def weight(l, at, first=0, n=D):
        parts = [w[l, :, :, pl.ds(at + 48 * k, 48), pl.ds(lane0, m)].reshape(D, m)
                 for k, lane0, m in pieces_of(first, n)]
        return parts[0] if len(parts) == 1 else jnp.concatenate(parts, axis=1)

    def put_grad_cols(l, at, first, val):
        done = 0
        for k, lane0, m in pieces_of(first, val.shape[1]):
            grad[l, :, :, pl.ds(at + 48 * k, 48), pl.ds(lane0, m)] = (
                val[:, done:done + m].astype(BF16).reshape(4, 2, 48, m))
            done += m

    def reduce_rows(l, first, n):
        got, at = [], first
        while at < first + n:
            m = min(192 - at % 192, first + n - at)
            s = at // 192
            got.append(w[l, s // 2, s % 2, pl.ds(REDUCE + at % 192, m), :])
            at += m
        return jnp.concatenate(got, axis=0)

    THIRDS = ((0, 512), (512, 512), (1024, 128))
    FW = 512


    plan = {}

    def during(phase, l, step, *calls):
        plan.setdefault((phase, l), {}).setdefault(step, []).extend(calls)

    def run(phase, l, n, body):
        at = plan.get((phase, l), {})

        def one(i, _):
            for step, calls in at.items():
                @pl.when(i == step)
                def _():
                    for call in calls:
                        call()
            body(i)
            return 0

        lax.fori_loop(0, n, one, 0)

    during("p1", 0, 0, F1.s1)
    during("p1", 0, 1, FF0.s4)
    during("p2", 0, 1, F1.s2)
    during("p3", 0, 0, F1.s3)
    during("p3", 0, 1, F1.s4)

    spills = [(g_s, g_spill, lsem.at[4]), (gp_s, gp_spill, lsem.at[5])]

    for l in range(2):
        if l:
            F1.done()
        acc = w[l, 0, 0, pl.ds(VEC, 16), :].astype(F32)
        for s in range(1, 8):
            acc = acc + w[l, s // 2, s % 2, pl.ds(VEC, 16), :].astype(F32)
        sp[l] = acc
        vec = lambda r: sp[l, r:r + 1, :]

        def p1(c):
            rows = rows_of(c)
            xhat, _r = normalize(xs[l, rows, :])
            a = (xhat * vec(0) + vec(1)).astype(BF16)
            a_s[l, rows, :] = a
            for first, n in THIRDS:
                val = dot(a, weight(l, JOINT, first, n))
                if first == 0:
                    val = jnp.concatenate([val[:, :D] * (HD ** -0.5), val[:, D:]], axis=1)
                qkv[l, rows, pl.ds(first, n)] = val.astype(BF16)

        run("p1", l, NCH, p1)

        def p2(k):
            heads = [(2 * k + u, j, e) for u in range(2) for j in range(3) for e in range(2)]
            scores, tops, weights, parts = [], [], [], []
            for i, j, e in heads:
                rows = img_rows(i)
                q2 = qkv[l, rows, pl.ds(128 * j, 128)]
                k2 = qkv[l, rows, pl.ds(D + 128 * j, 128)]
                scores.append(dot_nt(jnp.where(mine[e], k2, key_fill[e]),
                                     jnp.where(mine[e], q2, query_fill[e])))
            for st in scores:
                tops.append(jnp.max(st, axis=0, keepdims=True))
                weights.append(jnp.exp(st - tops[-1]).astype(BF16))
            for n, (i, j, e) in enumerate(heads):
                rows = img_rows(i)
                if e == 0:
                    v2t = qkv[l, rows, pl.ds(2 * D + 128 * j, 128)].T
                val = dot(jnp.concatenate([v2t[HD * e:HD * (e + 1), :], ones], axis=0), weights[n])
                tot = val[HD:HD + 1, :]
                lse_s[l, i, 2 * j + e:2 * j + e + 1, :] = tops[n] + jnp.log(tot)
                parts.append(val[:HD, :] * (1.0 / tot))
                if e == 1:
                    o_s[l, rows, pl.ds(128 * j, 128)] = jnp.concatenate(parts[-2:], axis=0).T.astype(BF16)

        run("p2", l, NI // 2, p2)

        if l == 0:
            FF0.done()
        else:
            for src, dst, sem in spills:
                pltpu.make_async_copy(src, dst, sem).wait()

        def p3(c):
            rows = rows_of(c)
            h = xs[l, rows, :] + dot(o_s[l, rows, :], weight(l, MERGE))
            hs[l, rows, :] = h
            xhat, _r = normalize(h)
            cc = (xhat * vec(2) + vec(3)).astype(BF16)
            c_s[l, rows, :] = cc
            acc = h + vec(4)
            bias = jnp.concatenate([vec(5 + k) for k in range(4)], axis=1)
            u, g = {}, {}
            for f in range(FF // FW + 2):
                if f < FF // FW:
                    u[f] = dot(cc, weight(l, EXPAND, FW * f, FW)) + bias[:, FW * f:FW * (f + 1)]
                if 1 <= f <= FF // FW:
                    val, slope = gelu_pair(u[f - 1])
                    g[f - 1] = val.astype(BF16)
                    g_s[rows, pl.ds(FW * (f - 1), FW)] = g[f - 1]
                    gp_s[rows, pl.ds(FW * (f - 1), FW)] = slope.astype(BF16)
                if f >= 2:
                    acc = acc + dot(g[f - 2], reduce_rows(l, FW * (f - 2), FW))
            if l == 0:
                xs[1, rows, :] = acc
            else:
                for k in range(CH // R):
                    i = c * (CH // R) + k
                    live = jnp.where(i < n_live, 1.0, 0.0).astype(F32)
                    dx_s[img_rows(i), :] = acc[R * k:R * (k + 1), :] * live

        run("p3", l, NCH, p3)
        if l == 0:
            for src, dst, sem in spills:
                pltpu.make_async_copy(src, dst, sem).start()

    put_out = pltpu.make_async_copy(dx_s, out, lsem.at[6])
    put_out.start()
    small[...] = jnp.zeros_like(small)
    get_cot.wait()
    put_out.wait()

    @pl.loop(0, NI)
    def _(i):
        live = jnp.where(i < n_live, 1.0, 0.0).astype(F32)
        dx_s[tail_rows(i), :] = jnp.zeros((16, D), F32)
        dx_s[img_rows(i, SEQ), :] = in_stage[i].astype(F32) * live

    R1, R2, R3, R4 = RD[1, FFN_ROWS], RD[1, ATT_ROWS], RD[0, FFN_ROWS], RD[0, ATT_ROWS]
    during("b2", 1, 1, R1.s1)
    during("b3", 1, 1, R1.s2)
    during("b1", 0, 1, R1.s3, R2.s1)
    during("b2", 0, 0, R1.s4, R2.s2)
    during("b2", 0, 1, R3.s1)
    during("b2", 0, 4, R2.s3)
    during("b3", 0, 1, R3.s2, R2.s4)

    def colsum(v):
        return jnp.sum(v, axis=0, keepdims=True)

    for l in (1, 0):
        vec = lambda r: sp[l, r:r + 1, :]
        if l == 0:
            for dst, src, sem in spills:
                pltpu.make_async_copy(src, dst, sem).wait()

        def b1(c):
            rows = rows_of(c)
            dx = dx_s[rows, :]
            dzb = dx.astype(BF16)
            dzb_s[rows, :] = dzb
            small[l, 4:5, :] += colsum(dzb.astype(F32))
            dg = {}
            for f in range(FF // FW + 1):
                if f < FF // FW:
                    dg[f] = dot_nt(dzb, reduce_rows(l, FW * f, FW))
                if f >= 1:
                    at = pl.ds(FW * (f - 1), FW)
                    gp_s[rows, at] = (dg[f - 1] * gp_s[rows, at].astype(F32)).astype(BF16)
            for k in range(4):
                small[l, 5 + k:6 + k, :] += colsum(gp_s[rows, pl.ds(D * k, D)].astype(F32))
            dc = dot_nt(gp_s[rows, :], weight(l, EXPAND, 0, FF))
            xhat, rstd = normalize(hs[l, rows, :])
            small[l, 2:3, :] += colsum(dc * xhat)
            small[l, 3:4, :] += colsum(dc)
            dh = dx + norm_back(dc, xhat, rstd, vec(2))
            dx_s[rows, :] = dh
            dyb = dh.astype(BF16)
            dyb_s[rows, :] = dyb
            hs[l, rows, :] = dot_nt(dyb, weight(l, MERGE))

        run("b1", l, NCH, b1)

        for f in range(FF // FW):
            put_grad_cols(l, EXPAND, FW * f, dot_tn(c_s[l], gp_s[:, pl.ds(FW * f, FW)]))
        for f in (0, 2):
            val = dot_tn(dzb_s[...], g_s[:, pl.ds(D * f, 2 * D)])
            grad[l, f, :, pl.ds(REDUCE, 192), :] = val[:, :D].T.astype(BF16).reshape(2, 192, D)
            grad[l, f + 1, :, pl.ds(REDUCE, 192), :] = val[:, D:].T.astype(BF16).reshape(2, 192, D)
        RD[l, FFN_ROWS].begin()
        if l:
            for dst, src, sem in spills:
                pltpu.make_async_copy(src, dst, sem).start()
        put_grad_cols(l, MERGE, 0, dot_tn(o_s[l], dyb_s[...]))

        def b2(i):
            rows = img_rows(i)
            heads = [(j, e) for j in range(3) for e in range(2)]
            scores, slopes, weights, down_scores = [], [], [], []
            dq, dk, dv, down = [], [], [], []
            for j, e in heads:
                q2 = qkv[l, rows, pl.ds(128 * j, 128)]
                k2 = qkv[l, rows, pl.ds(D + 128 * j, 128)]
                v2 = qkv[l, rows, pl.ds(2 * D + 128 * j, 128)]
                do2 = hs[l, rows, pl.ds(128 * j, 128)].astype(BF16)
                down.append(do2)
                scores.append(dot_nt(jnp.where(mine[e], k2, key_fill[e]),
                                     jnp.where(mine[e], q2, query_fill[e])))
                slopes.append(dot_nt(v2, jnp.where(mine[e], do2, blank)))
            for n, (j, e) in enumerate(heads):
                pt = jnp.exp(scores[n] - lse_s[l, i, n:n + 1, :])
                r = jnp.sum(slopes[n] * pt, axis=0, keepdims=True)
                weights.append(pt.astype(BF16))
                down_scores.append((pt * (slopes[n] - r)).astype(BF16))
            for n, (j, e) in enumerate(heads):
                if e == 0:
                    k2t = qkv[l, rows, pl.ds(D + 128 * j, 128)].T
                dv.append(dot(weights[n], down[n]))
                dk.append(dot(down_scores[n], qkv[l, rows, pl.ds(128 * j, 128)]))
                dq.append(dot(k2t[HD * e:HD * (e + 1), :], down_scores[n]))
                if e == 1:
                    new_q = jnp.concatenate(dq[-2:], axis=0).T * (HD ** -0.5)
                    qkv[l, rows, pl.ds(128 * j, 128)] = new_q.astype(BF16)
                    qkv[l, rows, pl.ds(D + 128 * j, 128)] = jnp.where(mine[0], *dk[-2:]).astype(BF16)
                    qkv[l, rows, pl.ds(2 * D + 128 * j, 128)] = jnp.where(mine[0], *dv[-2:]).astype(BF16)

        run("b2", l, NI, b2)

        def b3(c):
            rows = rows_of(c)
            da = dot_nt(qkv[l, rows, :], weight(l, JOINT, 0, 3 * D))
            xhat, rstd = normalize(xs[l, rows, :])
            small[l, 0:1, :] += colsum(da * xhat)
            small[l, 1:2, :] += colsum(da)
            dx = dx_s[rows, :] + norm_back(da, xhat, rstd, vec(0))
            dx_s[rows, :] = dx

        run("b3", l, NCH, b3)

        for s in range(8):
            grad[l, s // 2, s % 2, pl.ds(VEC, 16), :] = small[l].astype(BF16)
        for first, n in THIRDS:
            put_grad_cols(l, JOINT, first, dot_tn(a_s[l], qkv[l, :, pl.ds(first, n)]))
        RD[l, ATT_ROWS].begin()

    put_grad = pltpu.make_async_copy(dx_s, dimg, lsem.at[6])
    put_grad.start()
    R4.s1()
    R3.s3()
    for build in msgs.made[:3 * 29]:
        build().wait_send()
    R3.s4()
    R4.s2()
    R4.s3()
    R4.s4()
    for rd in (R1, R2, R3, R4):
        rd.done()
    put_total = pltpu.make_async_copy(total, total_out, lsem.at[7])
    put_total.start()
    for build in msgs.made[3 * 29:]:
        build().wait_send()
    put_grad.wait()
    put_total.wait()


def train(count, img, cot, joint, merge, expand, reduce_w, vec):
    A = pl.BlockSpec(memory_space=pl.ANY)
    vm = lambda *shape: pltpu.VMEM(shape, BF16)
    vf = lambda *shape: pltpu.VMEM(shape, F32)
    slots = []
    for k, n in enumerate((384, 256, 384, 256)):
        n4, n8, h = n // 4, n // 8, n // 2
        slots += [vm(4, 2, h, D) if k < 2 else vm(16, 128),
                  vm(3, 4, n4, 128), vm(3, n4, 128), vm(4, n4, 128),
                  vm(3, 4, 2, n8, 128), vm(3, 2, n8, 128), vm(2, n8, 128), vm(4, n8, 128),
                  vm(3, 2, h, 128), vm(4, h, 128), vm(4, h, 128), vm(16, 128)]
    return pl.pallas_call(
        train_kernel,
        out_shape=(
            jax.ShapeDtypeStruct((T, D), F32),
            jax.ShapeDtypeStruct((T, D), F32),
            jax.ShapeDtypeStruct((2, BLK, D), BF16),
            jax.ShapeDtypeStruct((T, FF), BF16),
            jax.ShapeDtypeStruct((T, FF), BF16),
        ),
        in_specs=[pl.BlockSpec(memory_space=pltpu.SMEM)] + [A] * 7,
        out_specs=(A,) * 5,
        scratch_shapes=[
            vm(2, 4, 2, BLK, D), vf(2, 16, D),
            vf(2, T, D), vf(2, T, D),
            vm(2, T, D), vm(2, T, D), vm(2, T, D),
            vm(2, T, 3 * D), vm(T, FF), vm(T, FF),
            vf(T, D), vm(T, D), vm(T, D),
            vf(2, NI, 8, R),
            vm(2, 4, 2, BLK, D), vf(2, 16, D), vm(2, BLK, D),
            vm(NI, SEQ, D),
            *slots,
            pltpu.SemaphoreType.DMA((N_SEMS,)), pltpu.SemaphoreType.DMA((N_SEMS,)),
            pltpu.SemaphoreType.DMA((8,)), pltpu.SemaphoreType.DMA((20,)),
        ],
        compiler_params=pltpu.CompilerParams(collective_id=0, has_side_effects=True,
                                             vmem_limit_bytes=65200 * 1024),
        cost_estimate=pl.CostEstimate(flops=28_000_000_000, bytes_accessed=20_000_000,
                                      transcendentals=8_000_000),
    )(count, img, cot, joint, merge, expand, reduce_w, vec)


N_SEMS = 3 * 29 + 4 * 50


BETA_ONE = 0.9
BETA_TWO = 0.999
ADAM_EPS = 1e-08
DECAY_MATRIX = 0.05
RATE_MATRIX = 0.05
RATE_SMALL = 0.4
STEP = 10


def adam_update(gradient, first_moment, second_moment, master, step_rate, decay_rate):
    first_new = BETA_ONE * first_moment + (1.0 - BETA_ONE) * gradient
    second_new = BETA_TWO * second_moment + (1.0 - BETA_TWO) * gradient * gradient
    corrected = first_new / (1.0 - BETA_ONE**STEP)
    denominator = jnp.sqrt(second_new / (1.0 - BETA_TWO**STEP)) + ADAM_EPS
    master_new = master - step_rate * (corrected / denominator + decay_rate * master)
    return (first_new, second_new, master_new)


def adam_kernel(g, rows_a, rows_b, *refs):
    ins, outs = refs[:12], refs[12:28]
    for src, dst in ((rows_a, refs[28]), (rows_b, refs[29])):
        dst[...] = src[:, :SEQ, :]
    for kind, (at, blocks, rows) in enumerate(
            [(JOINT, 3, 48), (MERGE, 1, 48), (EXPAND, 4, 48), (REDUCE, 1, 192)]):
        for cb in range(blocks):
            grad = g[0, pl.ds(at + 48 * cb, rows), :].astype(F32)
            cols = (0, slice(None), pl.ds(D * cb, D))
            m, v, wt = (ins[3 * kind + k][cols] for k in range(3))
            new = adam_update(grad, m, v, wt, RATE_MATRIX, DECAY_MATRIX)
            for k, val in enumerate((grad,) + new):
                outs[4 * kind + k][cols] = val


def adam(g, padded, firsts, seconds, masters):
    widths = (3 * D, D, 4 * D, D)
    rows = (48, 48, 48, 192)
    spec = [pl.BlockSpec((1, r, wd), lambda l: (l, 0, 0)) for r, wd in zip(rows, widths)]
    ins, in_specs, out_specs, shapes = [], [], [], []
    for k in range(4):
        for a in (firsts[k], seconds[k], masters[k]):
            ins.append(a)
            in_specs.append(spec[k])
        for _ in range(4):
            out_specs.append(spec[k])
            shapes.append(jax.ShapeDtypeStruct(masters[k].shape, F32))
    for _ in range(2):
        out_specs.append(pl.BlockSpec((NI // 2, SEQ, D), lambda l: (l, 0, 0)))
        shapes.append(jax.ShapeDtypeStruct((NI, SEQ, D), F32))
    return pl.pallas_call(
        adam_kernel,
        grid=(2,),
        out_shape=tuple(shapes),
        in_specs=[pl.BlockSpec((1, BLK, D), lambda l: (l, 0, 0))]
        + [pl.BlockSpec((NI // 2, R, D), lambda l: (l, 0, 0))] * 2 + in_specs,
        out_specs=tuple(out_specs),
        compiler_params=pltpu.CompilerParams(vmem_limit_bytes=60 * 1024 * 1024),
    )(g, *padded, *ins)


def shards(images, cotangent, image_count, joint_weight, merge_weight, expand_weight,
           reduce_weight, small_params, joint_first, merge_first, expand_first, reduce_first,
           small_first, joint_second, merge_second, expand_second, reduce_second, small_second):
    masters = (joint_weight, merge_weight, expand_weight, reduce_weight)
    firsts = (joint_first, merge_first, expand_first, reduce_first)
    seconds = (joint_second, merge_second, expand_second, reduce_second)
    width = small_params.shape[1]
    rank = lax.axis_index("shard")
    vec = lax.dynamic_update_slice_in_dim(jnp.zeros((2, 16 * D), F32), small_params, rank * width, 1)
    block_out, image_grad, total, _g, _gp = train(
        image_count, images, cotangent, *masters, vec.reshape(2, 16, D))
    done = adam(total, [v.reshape(NI, R, D) for v in (block_out, image_grad)], firsts, seconds, masters)
    vec_grad = lax.dynamic_slice_in_dim(total[:, VEC:VEC + 9].reshape(2, 9 * D), rank * width, width, 1)
    vec_grad = vec_grad.astype(F32)
    vec_done = (vec_grad,) + adam_update(vec_grad, small_first, small_second, small_params,
                                         RATE_SMALL, 0.0)
    outputs = list(done[16:])
    for member in range(4):
        outputs += [done[4 * kind + member] for kind in range(4)] + [vec_done[member]]
    return tuple(outputs)


def solution(mesh):
    whole = P(("replica", "shard"), None, None)
    weights = [P(None, "shard", None)] * 4 + [P(None, "shard")]
    return jax.shard_map(
        shards,
        mesh=mesh,
        in_specs=(whole, whole, P(("replica", "shard"))) + tuple(weights * 3),
        out_specs=(whole, whole) + tuple(weights * 4),
        check_vma=False,
    )
```
